32 devices in a mesh: dp: 2 (over core), blk: 16 (over z, y, x).
Axes of the slice: x: 2, y: 2, z: 4, core: 2. Of those that a mesh axis runs over, the one named last changes fastest.
Arguments:
- tokens: bfloat16 [2, 4096, 768], P('dp', 'blk'), may hold values from -6 to 6
- positions: int32 [2, 4096], P('dp', 'blk'), may hold values from 0 to 4095, as said below
- gain_attention: bfloat16 [768], P(('dp', 'blk')), may hold values from 0.5 to 1.5
- bias_attention: bfloat16 [768], P(('dp', 'blk')), may hold values from -1.5 to 1.5
- gain_feed: bfloat16 [768], P(('dp', 'blk')), may hold values from 0.5 to 1.5
- bias_feed: bfloat16 [768], P(('dp', 'blk')), may hold values from -1.5 to 1.5
- weight_joined: bfloat16 [768, 2304], P(('dp', 'blk')), may hold values from -0.3125 to 0.3125
- bias_joined: bfloat16 [2304], P(('dp', 'blk')), may hold values from -3 to 3
- weight_merge: bfloat16 [768, 768], P(('dp', 'blk')), may hold values from -0.875 to 0.875
- bias_merge: bfloat16 [768], P(('dp', 'blk')), may hold values from -1.5 to 1.5
- weight_expand: bfloat16 [768, 3072], P(('dp', 'blk')), may hold values from -0.21875 to 0.21875
- bias_expand: bfloat16 [3072], P(('dp', 'blk')), may hold values from -3 to 3
- weight_reduce: bfloat16 [3072, 768], P(('dp', 'blk')), may hold values from -0.109375 to 0.109375
- bias_reduce: bfloat16 [768], P(('dp', 'blk')), may hold values from -1.5 to 1.5
- cotangent: bfloat16 [2, 4096, 768], P('dp', 'blk'), may hold values from -6 to 6
Outputs:
- result: bfloat16 [2, 4096, 768], P('dp', 'blk')
- gradient_tokens: float32 [2, 4096, 768], P('dp', 'blk')
- gradient_gain_attention: float32 [768], P(('dp', 'blk'))
- gradient_bias_attention: float32 [768], P(('dp', 'blk'))
- gradient_gain_feed: float32 [768], P(('dp', 'blk'))
- gradient_bias_feed: float32 [768], P(('dp', 'blk'))
- gradient_weight_joined: float32 [768, 2304], P(('dp', 'blk'))
- gradient_bias_joined: float32 [2304], P(('dp', 'blk'))
- gradient_weight_merge: float32 [768, 768], P(('dp', 'blk'))
- gradient_bias_merge: float32 [768], P(('dp', 'blk'))
- gradient_weight_expand: float32 [768, 3072], P(('dp', 'blk'))
- gradient_bias_expand: float32 [3072], P(('dp', 'blk'))
- gradient_weight_reduce: float32 [3072, 768], P(('dp', 'blk'))
- gradient_bias_reduce: float32 [768], P(('dp', 'blk'))
The draws below stay inside these ranges and needn't reach their ends.
Inputs may be any that keep to these rules, and one draw needn't show every extreme that they name: Each row is a permutation of the positions of one sequence, made of runs of 128 ascending consecutive positions, each run starting at a multiple of 128.
All inputs are finite; a program needn't handle non-finite values.
Results may differ from the reference program's by a relative error of at most 0.014.
Values may be sent and summed in bfloat16 or wider, within the bound.
No kernel may reach another device: no remote copies, remote signals or barrier semaphores. Data moves between devices by JAX's collectives and lax.ppermute only.
A program may use at most 128 MiB of HBM per device.

```python
import math
import jax
import jax.numpy as jnp
from jax import lax

D = 768
H = 12
HD = 64
FF = 3072
ROT = 16
BLK_TOK = 256
LEN = 4096
NSEQ = 2


def draw_positions(key, part):
    key = jax.random.fold_in(key, 11)
    half_rows = BLK_TOK // 2
    pieces = LEN // half_rows
    subkeys = jax.random.split(key, NSEQ)

    def shuffle(subkey):
        return jax.random.permutation(subkey, pieces)
    order = jax.vmap(shuffle)(subkeys).astype(jnp.int32)
    offsets = jnp.arange(half_rows, dtype=jnp.int32)
    return (order[:, :, None] * half_rows + offsets[None, None, :]).reshape(NSEQ, LEN).astype(jnp.int32)


def level_of(key, extent, shards, least, top_value):
    def one(axis_at, shards_of):
        steps = jax.random.uniform(jax.random.fold_in(jax.random.fold_in(key, 6), axis_at), (shards_of,), jnp.float32, least / len(shards), top_value / len(shards))
        return jnp.repeat(jnp.exp(steps), extent[axis_at] // shards_of).reshape((-1,) + (1,) * (len(extent) - axis_at - 1))

    loudness = one(*shards[0])
    for cut in shards[1:]:
        loudness = loudness * one(*cut)
    return loudness


def gaussian(stream_key, shape, deviation, reach, cuts=(), held_as=jnp.bfloat16):
    drawn = deviation * jax.random.normal(stream_key, shape, jnp.float32)
    if cuts:
        drawn = drawn * level_of(stream_key, shape, cuts, -0.22, 0.18)
    return jnp.clip(drawn, -reach, reach).astype(held_as)


def setup_inputs(seed: int = 0) -> dict:
    streams_of = jax.random.split(jax.random.key(seed), 16)
    return {
        "tokens": gaussian(streams_of[0], (NSEQ, LEN, D), 1.0, 6.0, ((0, 2), (1, 16))),
        "positions": draw_positions(jax.random.fold_in(streams_of[15], 71), 0),
        "gain_attention": jnp.clip(1.0 + 0.1 * jax.random.normal(streams_of[2], (D,), jnp.float32), 0.5, 1.5).astype(jnp.bfloat16),
        "bias_attention": gaussian(streams_of[3], (D,), 0.3, 1.5, ((0, 32),)),
        "gain_feed": jnp.clip(1.0 + 0.1 * jax.random.normal(streams_of[4], (D,), jnp.float32), 0.5, 1.5).astype(jnp.bfloat16),
        "bias_feed": gaussian(streams_of[5], (D,), 0.3, 1.5, ((0, 32),)),
        "weight_joined": gaussian(streams_of[6], (D, 3 * D), (D // 2) ** -0.5, 0.3125, ((0, 32),)),
        "bias_joined": gaussian(streams_of[7], (3 * D,), 0.5, 3.0, ((0, 32),)),
        "weight_merge": gaussian(streams_of[8], (D, D), (D // 16) ** -0.5, 0.875, ((0, 32),)),
        "bias_merge": gaussian(streams_of[9], (D,), 0.3, 1.5, ((0, 32),)),
        "weight_expand": gaussian(streams_of[10], (D, FF), D ** -0.5, 0.21875, ((0, 32),)),
        "bias_expand": gaussian(streams_of[11], (FF,), 0.5, 3.0, ((0, 32),)),
        "weight_reduce": gaussian(streams_of[12], (FF, D), FF ** -0.5, 0.109375, ((0, 32),)),
        "bias_reduce": gaussian(streams_of[13], (D,), 0.3, 1.5, ((0, 32),)),
        "cotangent": gaussian(streams_of[14], (NSEQ, LEN, D), 1.0, 6.0, ((0, 2), (1, 16))),
    }


highest = lax.Precision.HIGHEST
norm_eps = 1e-05
masked_score = -1e+30

@jax.custom_vjp
def low(v):
    return lax.optimization_barrier(v.astype(jnp.bfloat16)).astype(jnp.float32)

@jax.custom_vjp
def low_back(v):
    return v

def low_keep(v):
    return (low(v), None)

def low_pass(kept, grad):
    return (grad,)

def back_keep(v):
    return (v, None)

def back_low(kept, grad):
    return (low(grad),)
low.defvjp(low_keep, low_pass)
low_back.defvjp(back_keep, back_low)

def layer_norm(values, gain, shift):
    middle = lax.optimization_barrier(jnp.mean(values, axis=-1, keepdims=True))
    centred = values - middle
    spread = lax.optimization_barrier(jnp.mean(centred * centred, axis=-1, keepdims=True))
    return centred * lax.rsqrt(spread + norm_eps) * gain + shift

def rotate(values, places):
    half_dims = ROT // 2
    frequency = jnp.exp(jnp.arange(half_dims, dtype=jnp.float32) * (-2.0 * math.log(10000.0) / ROT))
    angles = places[..., None] * frequency
    cosine = jnp.cos(angles)[..., None, :]
    sine = jnp.sin(angles)[..., None, :]
    first = values[..., :half_dims]
    second = values[..., half_dims:ROT]
    return jnp.concatenate([first * cosine - second * sine, second * cosine + first * sine, values[..., ROT:]], axis=-1)

def attend_one(item):
    queries, keys, values, places = item
    scores = jnp.einsum('qhd,khd->hqk', queries, keys, precision=highest) * HD ** (-0.5)
    scores = low_back(scores)
    visible = places[None, :] <= places[:, None]
    scores = jnp.where(visible[None], scores, masked_score)
    chances = low(jax.nn.softmax(scores, axis=-1))
    return jnp.einsum('hqk,khd->qhd', chances, values, precision=highest)

def forward(inputs, positions, gain_attention, bias_attention, gain_feed, bias_feed, weight_joined, bias_joined, weight_merge, bias_merge, weight_expand, bias_expand, weight_reduce, bias_reduce):
    count, length = (inputs.shape[0], inputs.shape[1])
    rows = inputs.reshape(-1, D)
    first_norm = low(layer_norm(rows, gain_attention, bias_attention))
    second_norm = low(layer_norm(rows, gain_feed, bias_feed))
    joined = low_back(jnp.dot(first_norm, weight_joined, precision=highest) + bias_joined)
    places = positions.astype(jnp.float32)
    head_shape = (count, length, H, HD)
    queries = low(rotate(joined[:, :D].reshape(head_shape), places))
    keys = low(rotate(joined[:, D:2 * D].reshape(head_shape), places))
    values = low(joined[:, 2 * D:].reshape(head_shape))
    attended = lax.map(jax.checkpoint(attend_one), (queries, keys, values, positions))
    attended = low(low_back(attended.reshape(-1, D)))
    branch_attention = jnp.dot(attended, weight_merge, precision=highest) + bias_merge
    expanded = low_back(jnp.dot(second_norm, weight_expand, precision=highest) + bias_expand)
    active = low(jax.nn.gelu(expanded, approximate=False))
    branch_feed = jnp.dot(active, weight_reduce, precision=highest) + bias_reduce
    return (rows + branch_attention + branch_feed).reshape(inputs.shape)

def reference(tokens, positions, gain_attention, bias_attention, gain_feed, bias_feed, weight_joined, bias_joined, weight_merge, bias_merge, weight_expand, bias_expand, weight_reduce, bias_reduce, cotangent):
    params = tuple((piece.astype(jnp.float32) for piece in (gain_attention, bias_attention, gain_feed, bias_feed, weight_joined, bias_joined, weight_merge, bias_merge, weight_expand, bias_expand, weight_reduce, bias_reduce)))

    def wrapped(inputs, *weights):
        return forward(inputs, positions, *weights)
    output, pullback = jax.vjp(wrapped, tokens.astype(jnp.float32), *params)
    grads = pullback(cotangent.astype(jnp.float32))
    return (output.astype(jnp.bfloat16), grads[0], grads[1], grads[2], grads[3], grads[4], grads[5], grads[6], grads[7], grads[8], grads[9], grads[10], grads[11], grads[12])
```

```python
import functools
import math

import jax
import jax.numpy as jnp
from jax import lax
from jax.experimental import pallas as pl
from jax.experimental.pallas import tpu as pltpu
from jax.sharding import PartitionSpec as P

HD = 64
ROT = 16
TP = 4
RUN = 128
TILE = 2 * RUN
KEYS = 256

norm_eps = 1e-05
masked_score = -1e30
low = jnp.bfloat16
full = jnp.float32


def dot(a, b, dims=((1,), (0,))):
    return lax.dot_general(a, b, (dims, ((), ())), preferred_element_type=full)


def attention_kernel(
    heads, groups, runs, q_runs_ref, q_order_ref, k_runs_ref, q_ref, o_grad_ref, *refs
):
    kv_refs = refs[:groups]
    out_ref, q_grad_ref = refs[groups : groups + 2]
    kv_grad_refs = refs[groups + 2 : 2 * groups + 2]
    kv, kv_turned, total, first_w, second_w, state, out_total, q_total = refs[2 * groups + 2 :]
    pair = 2 * HD

    for source in range(groups):

        def place(run, carry, source=source):
            at = pl.multiple_of(k_runs_ref[source * runs + run] * RUN, RUN)
            rows = kv_refs[source][pl.ds(pl.multiple_of(run * RUN, RUN), RUN), :]
            kv[pl.ds(at, RUN), :] = rows
            for head in range(heads):
                part = slice(head * pair, (head + 1) * pair)
                kv_turned[part, pl.ds(at, RUN)] = rows[:, part].T
            total[pl.ds(at, RUN), :] = jnp.zeros((RUN, heads * pair), full)
            return carry

        lax.fori_loop(0, runs, place, 0)

    def tile_step(tile, carry):
        early, late = q_order_ref[2 * tile], q_order_ref[2 * tile + 1]
        early_run, late_run = q_runs_ref[early], q_runs_ref[late]
        early_rows = pl.ds(pl.multiple_of(early * RUN, RUN), RUN)
        late_rows = pl.ds(pl.multiple_of(late * RUN, RUN), RUN)

        def rows_of(ref):
            return jnp.concatenate([ref[early_rows, :], ref[late_rows, :]], axis=0)

        queries, o_grads = rows_of(q_ref), rows_of(o_grad_ref)
        lane = lax.broadcasted_iota(jnp.int32, (TILE, pair), 1)
        for head in range(heads):
            part = slice(head * HD, (head + 1) * HD)
            both = jnp.concatenate([queries[:, part], o_grads[:, part]], axis=1)
            upper = jnp.where(lane < HD, both, jnp.zeros_like(both))
            lower = jnp.where(lane >= HD, both, jnp.zeros_like(both))
            second_w[head, :TILE, :] = upper
            second_w[head, TILE:, :] = lower
            first_w[head, :, :TILE] = upper.T
            first_w[head, :, TILE:] = lower.T

        column = lax.broadcasted_iota(jnp.int32, (1, TILE), 1)
        q_places = jnp.where(column < RUN, early_run * RUN + column, late_run * RUN + column - RUN)
        seen_by_all = lax.div(early_run * RUN, KEYS)
        seen = lax.div(late_run * RUN + RUN + KEYS - 1, KEYS)

        state[...] = jnp.full(state.shape, masked_score, full)
        out_total[...] = jnp.zeros_like(out_total)
        q_total[...] = jnp.zeros_like(q_total)

        def masked(scores, block):
            k_places = block * KEYS + lax.broadcasted_iota(jnp.int32, (KEYS, TILE), 0)
            return jnp.where(k_places <= q_places, scores, masked_score)

        def forward(hides, block, sums):
            rows = pl.ds(pl.multiple_of(block * KEYS, KEYS), KEYS)
            new_sums = []
            for head in range(heads):
                part = slice(head * pair, (head + 1) * pair)
                scores = dot(kv[rows, part], first_w[head, :, :TILE])
                if hides:
                    scores = masked(scores, block)
                old_max = state[head : head + 1, :]
                new_max = jnp.maximum(old_max, jnp.max(scores, axis=0, keepdims=True))
                weights = jnp.exp(scores - new_max)
                fading = jnp.exp(old_max - new_max)
                state[head : head + 1, :] = new_max
                new_sums.append(sums[head] * fading + jnp.sum(weights, axis=0, keepdims=True))
                here = slice(head * HD, (head + 1) * HD)
                added = dot(
                    kv_turned[head * pair + HD : (head + 1) * pair, rows], weights.astype(low)
                )
                out_total[here, :] = out_total[here, :] * fading + added
            return tuple(new_sums)

        sums = tuple(jnp.zeros((1, TILE), full) for _ in range(heads))
        sums = lax.fori_loop(0, seen_by_all, functools.partial(forward, False), sums)
        sums = lax.fori_loop(seen_by_all, seen, functools.partial(forward, True), sums)

        log_totals, deltas = [], []
        for head in range(heads):
            here = slice(head * HD, (head + 1) * HD)
            attended = out_total[here, :] / sums[head]
            out_total[here, :] = attended
            log_totals.append(state[head : head + 1, :] + jnp.log(sums[head]))
            o_grad = first_w[head, HD:, TILE:].astype(full)
            deltas.append(jnp.sum(o_grad * attended, axis=0, keepdims=True))
        attended = out_total[...].T.astype(low)
        out_ref[early_rows, :] = attended[:RUN]
        out_ref[late_rows, :] = attended[RUN:]

        def backward(hides, block, carry):
            rows = pl.ds(pl.multiple_of(block * KEYS, KEYS), KEYS)
            for head in range(heads):
                part = slice(head * pair, (head + 1) * pair)
                both = dot(kv[rows, part], first_w[head])
                scores = both[:, :TILE]
                if hides:
                    scores = masked(scores, block)
                chances = jnp.exp(scores - log_totals[head])
                score_grad = (chances * (both[:, TILE:] - deltas[head])).astype(low)
                joint = jnp.concatenate([score_grad, chances.astype(low)], axis=1)
                total[rows, part] += dot(joint, second_w[head])
                here = slice(head * HD, (head + 1) * HD)
                q_total[here, :] += dot(kv_turned[head * pair : head * pair + HD, rows], score_grad)
            return carry

        lax.fori_loop(0, seen_by_all, functools.partial(backward, False), 0)
        lax.fori_loop(seen_by_all, seen, functools.partial(backward, True), 0)
        q_grad = q_total[...].T
        q_grad_ref[early_rows, :] = q_grad[:RUN]
        q_grad_ref[late_rows, :] = q_grad[RUN:]
        return carry

    lax.fori_loop(0, q_ref.shape[0] // TILE, tile_step, 0)

    for source in range(groups):

        def give(run, carry, source=source):
            at = pl.multiple_of(k_runs_ref[source * runs + run] * RUN, RUN)
            rows = pl.ds(pl.multiple_of(run * RUN, RUN), RUN)
            kv_grad_refs[source][rows, :] = total[pl.ds(at, RUN), :].astype(low)
            return carry

        lax.fori_loop(0, runs, give, 0)


def attention(queries, o_grads, q_runs, q_order, kv_parts, k_runs):
    groups = len(kv_parts)
    count, width = queries.shape
    heads = width // HD
    runs = count // RUN
    keys = groups * count
    smem = pl.BlockSpec(memory_space=pltpu.SMEM)
    vmem = pl.BlockSpec(memory_space=pltpu.VMEM)
    kv_shape = jax.ShapeDtypeStruct((count, 2 * width), low)
    pairs = count * keys * heads
    out = pl.pallas_call(
        functools.partial(attention_kernel, heads, groups, runs),
        out_shape=(
            jax.ShapeDtypeStruct((count, width), low),
            jax.ShapeDtypeStruct((count, width), full),
        )
        + (kv_shape,) * groups,
        in_specs=[smem] * 3 + [vmem] * (2 + groups),
        out_specs=tuple([vmem] * (2 + groups)),
        scratch_shapes=[
            pltpu.VMEM((keys, 2 * width), low),
            pltpu.VMEM((2 * width, keys), low),
            pltpu.VMEM((keys, 2 * width), full),
            pltpu.VMEM((heads, 2 * HD, 2 * TILE), low),
            pltpu.VMEM((heads, 2 * TILE, 2 * HD), low),
            pltpu.VMEM((8, TILE), full),
            pltpu.VMEM((width, TILE), full),
            pltpu.VMEM((width, TILE), full),
        ],
        compiler_params=pltpu.CompilerParams(vmem_limit_bytes=(12 + 9 * groups // 2) * 2**20),
        cost_estimate=pl.CostEstimate(
            flops=7 * HD * pairs, bytes_accessed=16 * count * width * groups, transcendentals=pairs
        ),
        name="attention",
    )(q_runs, q_order, k_runs, queries, o_grads, *kv_parts)
    return out[0], out[1], out[2:]


def rotation_tables(places, columns):
    half_dims = ROT // 2
    frequency = jnp.exp(jnp.arange(half_dims, dtype=full) * (-2.0 * math.log(10000.0) / ROT))
    angles = places[:, None] * frequency
    cosine, sine = jnp.cos(angles), jnp.sin(angles)
    rest = (places.shape[0], HD - ROT)
    cosines = jnp.concatenate([cosine, cosine, jnp.ones(rest, full)], axis=1)
    sines = jnp.concatenate([-sine, sine, jnp.zeros(rest, full)], axis=1)
    return jnp.tile(cosines, (1, columns // HD)), jnp.tile(sines, (1, columns // HD))


def partners(values):
    half_dims = ROT // 2
    lane = lax.broadcasted_iota(jnp.int32, values.shape, 1) % HD
    return jnp.where(
        lane < half_dims, jnp.roll(values, -half_dims, axis=1), jnp.roll(values, half_dims, axis=1)
    )


def on_device(
    tokens,
    positions,
    gain_attention,
    bias_attention,
    gain_feed,
    bias_feed,
    weight_joined,
    bias_joined,
    weight_merge,
    bias_merge,
    weight_expand,
    bias_expand,
    weight_reduce,
    bias_reduce,
    cotangent,
):
    seqs, block, width = tokens.shape
    units = weight_expand.shape[1]
    copies = lax.axis_size("dp")
    members = lax.axis_size("blk")
    groups = members // TP
    here = lax.axis_index("blk")
    my_part, my_group, my_copy = here // groups, here % groups, lax.axis_index("dp")
    heads = width // HD // TP
    depth = weight_joined.shape[0]
    part_units = units // TP
    my_units = weight_reduce.shape[0]
    span = heads * HD

    def over_parts(value, away):
        return lax.ppermute(value, "blk", [(i, i ^ (away * groups)) for i in range(members)])

    def over_groups(value, away):
        return lax.ppermute(value, "blk", [(i, i ^ away) for i in range(members)])

    def over_copies(value, away):
        return lax.ppermute(value, "dp", [(i, i ^ away) for i in range(copies)])

    def placed(pieces, me):
        out = jnp.zeros((len(pieces),) + pieces[0].shape, pieces[0].dtype)
        for away, piece in enumerate(pieces):
            out = lax.dynamic_update_index_in_dim(out, piece, me ^ away, 0)
        return out

    def gathered(value, move, count, me):
        return placed([value] + [move(value, away) for away in range(1, count)], me)

    def picked(value, at, axis):
        return lax.dynamic_index_in_dim(value, at, axis, keepdims=False)

    def exchanged(value, move, count, me, axis):
        return [picked(value, me, axis)] + [
            move(picked(value, me ^ away, axis), away) for away in range(1, count)
        ]

    def added(pieces):
        return functools.reduce(jnp.add, [piece.astype(full) for piece in pieces])

    def whole_rows(value):
        value = gathered(value, over_groups, groups, my_group)
        value = gathered(value, over_copies, copies, my_copy)
        return jnp.swapaxes(value, 1, 2)

    def of_group(value):
        return jnp.concatenate([value] + [over_parts(value, away) for away in range(1, TP)], axis=0)

    places = of_group(positions.reshape(block))
    rows_low = of_group(tokens.reshape(block, width))
    rows = rows_low.astype(full)
    count = rows.shape[0]
    runs = count // RUN

    vectors = (
        gain_attention,
        bias_attention,
        gain_feed,
        bias_feed,
        bias_merge,
        bias_reduce,
        bias_joined,
        bias_expand,
    )
    small = jnp.concatenate(vectors)

    def by_head(matrix):
        lead = matrix.shape[:-1]
        split = matrix.reshape(lead + (3, TP, heads, HD))
        queries = split[..., 0, :, :, :].reshape(lead + (TP, span))
        kv = jnp.stack([split[..., 1, :, :, :], split[..., 2, :, :, :]], axis=-2)
        return jnp.concatenate([queries, kv.reshape(lead + (TP, 2 * span))], axis=-1)

    def from_head(matrix):
        lead = matrix.shape[:-2]
        queries = matrix[..., :span].reshape(lead + (1, TP, heads, HD))
        kv = matrix[..., span:].reshape(lead + (TP, heads, 2, HD))
        kv = jnp.moveaxis(kv, -2, len(lead))
        return jnp.concatenate([queries, kv], axis=len(lead)).reshape(lead + (3 * width,))

    joined_parts = jnp.swapaxes(by_head(weight_joined), 0, 1)
    padding = jnp.zeros((3 * span - small.shape[0],), low)
    small_row = jnp.broadcast_to(jnp.concatenate([small, padding]), (TP, 1, 3 * span))
    joined_parts = jnp.concatenate([joined_parts, small_row], axis=1)
    joined_all = whole_rows(placed(exchanged(joined_parts, over_parts, TP, my_part, 0), my_part))
    joined_matrix = joined_all[..., :depth, :].reshape(width, 3 * span)
    small_all = joined_all[..., depth, : small.shape[0]].astype(full)
    pieces = []
    start = 0
    for vector in vectors:
        pieces.append(small_all[..., start : start + vector.shape[0]])
        start += vector.shape[0]
    gain_one, shift_one, gain_two, shift_two, merge_shift, reduce_shift, joined_shift = [
        piece.reshape(-1) for piece in pieces[:7]
    ]
    joined_shift = picked(by_head(joined_shift), my_part, 0)
    expand_shift = picked(pieces[7], my_part, 1).reshape(-1)

    expand_split = weight_expand.reshape(depth, copies, TP, groups * my_units)
    expand_parts = jnp.moveaxis(expand_split, 2, 0).reshape(TP, depth, part_units)
    merge_parts = jnp.broadcast_to(weight_merge, (TP, depth, width))
    later_parts = jnp.concatenate([expand_parts, merge_parts], axis=2)
    later_all = whole_rows(placed(exchanged(later_parts, over_parts, TP, my_part, 0), my_part))
    expand_matrix = later_all[..., :part_units].reshape(width, part_units)
    merge_matrix = later_all[..., part_units:].reshape(width, width)
    merge_matrix = lax.dynamic_slice_in_dim(merge_matrix, my_part * span, span, 0)
    reduce_matrix = gathered(weight_reduce, over_groups, groups, my_group)
    reduce_matrix = gathered(reduce_matrix, over_copies, copies, my_copy)
    reduce_matrix = reduce_matrix.reshape(part_units, width)

    middle = jnp.mean(rows, axis=-1, keepdims=True)
    centred = rows - middle
    inverse = lax.rsqrt(jnp.mean(centred * centred, axis=-1, keepdims=True) + norm_eps)
    normed = centred * inverse
    first_low = (normed * gain_one + shift_one).astype(low)
    second_low = (normed * gain_two + shift_two).astype(low)
    joined = dot(first_low, joined_matrix) + joined_shift
    cosines, sines = rotation_tables(places.astype(full), 3 * span)
    column = lax.broadcasted_iota(jnp.int32, (1, 3 * span), 1)
    is_value = (column >= span) & ((column - span) % (2 * HD) >= HD)
    cosines = jnp.where(is_value, 1.0, cosines)
    sines = jnp.where(is_value, 0.0, sines)
    turned = (joined * cosines + partners(joined) * sines).astype(low)
    queries = turned[:, :span] * jnp.asarray(HD**-0.5, low)
    kv = turned[:, span:]
    q_runs = places[::RUN] // RUN
    rank = jnp.sum(q_runs[None, :] < q_runs[:, None], axis=1)
    index = jnp.arange(runs, dtype=jnp.int32)
    q_order = jnp.sum(jnp.where(rank[None, :] == index[:, None], index[None, :], 0), axis=1)
    kv_parts = [kv] + [over_groups(kv, away) for away in range(1, groups)]
    k_runs = jnp.concatenate([q_runs] + [over_groups(q_runs, away) for away in range(1, groups)])

    upstream_low = of_group(cotangent.reshape(block, width))
    attended_gradient = dot(upstream_low, merge_matrix, ((1,), (1,))).astype(low)

    attended_low, query_total, kv_totals = attention(
        queries, attended_gradient, q_runs, q_order.astype(jnp.int32), kv_parts, k_runs
    )

    expanded = dot(second_low, expand_matrix) + expand_shift
    active, gelu_pull = jax.vjp(lambda v: jax.nn.gelu(v, approximate=False), expanded)
    active_low = active.astype(low)
    active_gradient = dot(upstream_low, reduce_matrix, ((1,), (1,)))
    expanded_gradient = gelu_pull(active_gradient)[0].astype(low)
    second_gradient = dot(expanded_gradient, expand_matrix, ((1,), (1,)))

    def of_rows(partial):
        chunks = partial.astype(low).reshape(TP, block, width)
        mine = partial.reshape(TP, block, width)[0]
        return added([mine] + [over_parts(chunks[away], away) for away in range(1, TP)])

    branches = of_rows(dot(active_low, reduce_matrix) + dot(attended_low, merge_matrix))
    result = (rows[:block] + branches + merge_shift + reduce_shift).astype(low)

    def over_all(value):
        value = added(exchanged(value.astype(low), over_copies, copies, my_copy, 0))
        return added(exchanged(value.astype(low), over_groups, groups, my_group, 1))

    def by_rows(matrix):
        return matrix.reshape((copies, TP, groups, depth) + matrix.shape[1:])

    gradient_weight_expand = over_all(by_rows(dot(second_low, expanded_gradient, ((0,), (0,)))))
    gradient_weight_expand = placed(
        exchanged(gradient_weight_expand.astype(low), over_parts, TP, my_part, 0), my_part
    )
    gradient_weight_expand = jnp.moveaxis(
        gradient_weight_expand.reshape(TP, depth, copies, groups * my_units), 0, 2
    ).reshape(depth, units)
    gradient_weight_reduce = over_all(
        dot(active_low, upstream_low, ((0,), (0,))).reshape(copies, 1, groups, my_units, width)
    )[0]
    merge_rows = dot(attended_low, upstream_low, ((0,), (0,)))
    merge_rows = lax.dynamic_update_slice_in_dim(
        jnp.zeros((width, width), full), merge_rows, my_part * span, 0
    )
    gradient_weight_merge = added(
        exchanged(over_all(by_rows(merge_rows)).astype(low), over_parts, TP, my_part, 0)
    )

    kv_total = added([kv_totals[0]] + [over_groups(kv_totals[r], r) for r in range(1, groups)])
    joined_total = jnp.concatenate([query_total * HD**-0.5, kv_total], axis=1)
    joined_gradient = (joined_total * cosines - partners(joined_total) * sines).astype(low)
    first_gradient = dot(joined_gradient, joined_matrix, ((1,), (1,)))
    slope = first_gradient * gain_one + second_gradient * gain_two
    slope = of_rows(slope)
    own = normed[:block]
    upstream = cotangent.reshape(block, width).astype(full)
    gradient_tokens = upstream + inverse[:block] * (
        slope
        - jnp.mean(slope, axis=-1, keepdims=True)
        - own * jnp.mean(slope * own, axis=-1, keepdims=True)
    )

    sums = (
        jnp.sum(first_gradient * normed, axis=0),
        jnp.sum(first_gradient, axis=0),
        jnp.sum(second_gradient * normed, axis=0),
        jnp.sum(second_gradient, axis=0),
        jnp.sum(upstream, axis=0),
    )
    shape = (copies, TP, groups)
    joined_sum = jnp.sum(joined_gradient.astype(full), axis=0)
    joined_sum = from_head(placed_alone(joined_sum, my_part, TP))
    expand_sum = jnp.sum(expanded_gradient.astype(full), axis=0).reshape(copies, groups, my_units)
    expand_sum = jnp.swapaxes(placed_alone(expand_sum, my_part, TP), 0, 1)
    small_sums = jnp.concatenate(
        [piece.reshape(shape + (depth,)) for piece in sums]
        + [joined_sum.reshape(shape + (3 * depth,)), expand_sum],
        axis=-1,
    )
    padding = jnp.zeros(shape + (3 * span - small_sums.shape[-1],), full)
    small_sums = jnp.concatenate([small_sums, padding], axis=-1)[..., None, :]
    joined_rows = by_rows(dot(first_low, joined_gradient, ((0,), (0,))))
    final = over_all(jnp.concatenate([joined_rows, small_sums], axis=-2))
    final = exchanged(final.astype(low), over_parts, TP, my_part, 0)
    gradient_weight_joined = placed([piece[:depth] for piece in final], my_part)
    gradient_weight_joined = from_head(jnp.swapaxes(gradient_weight_joined, 0, 1))
    small_total = added([piece[depth] for piece in final])
    gradients = [small_total[k * depth : (k + 1) * depth] for k in range(5)]
    gradient_bias_joined = small_total[5 * depth : 8 * depth]
    gradient_bias_expand = small_total[8 * depth : 8 * depth + my_units]

    def wide(value):
        return value.astype(full)

    return (
        result.reshape(tokens.shape),
        gradient_tokens.reshape(tokens.shape),
        gradients[0],
        gradients[1],
        gradients[2],
        gradients[3],
        wide(gradient_weight_joined),
        gradient_bias_joined,
        wide(gradient_weight_merge),
        gradients[4],
        wide(gradient_weight_expand),
        gradient_bias_expand,
        wide(gradient_weight_reduce),
        gradients[4],
    )


def placed_alone(value, at, count):
    out = jnp.zeros((count,) + value.shape, value.dtype)
    return lax.dynamic_update_index_in_dim(out, value, at, 0)


def solution(mesh):
    rows = P("dp", "blk", None)
    vector, matrix = P(("dp", "blk")), P(("dp", "blk"), None)
    params = (vector,) * 4 + (matrix, vector) * 4
    return jax.shard_map(
        on_device,
        mesh=mesh,
        in_specs=(rows, P("dp", "blk")) + params + (rows,),
        out_specs=(rows, rows) + params,
        check_vma=False,
    )
```

```python
import functools
import math

import jax
import jax.numpy as jnp
from jax import lax
from jax.experimental import pallas as pl
from jax.experimental.pallas import tpu as pltpu
from jax.sharding import PartitionSpec as P

HD = 64
ROT = 16
TP = 4
RUN = 128
TILE = 2 * RUN
KEYS = 256

norm_eps = 1e-05
masked_score = -1e30
low = jnp.bfloat16
full = jnp.float32


def dot(a, b, dims=((1,), (0,))):
    return lax.dot_general(a, b, (dims, ((), ())), preferred_element_type=full)


def tile_of(tile, q_runs_ref, q_order_ref):
    early, late = q_order_ref[2 * tile], q_order_ref[2 * tile + 1]
    early_run, late_run = q_runs_ref[early], q_runs_ref[late]
    rows = [pl.ds(pl.multiple_of(run * RUN, RUN), RUN) for run in (early, late)]
    column = lax.broadcasted_iota(jnp.int32, (1, TILE), 1)
    places = jnp.where(column < RUN, early_run * RUN + column, late_run * RUN + column - RUN)
    seen_by_all = lax.div(early_run * RUN, KEYS)
    seen = lax.div(late_run * RUN + RUN + KEYS - 1, KEYS)
    return rows, places, seen_by_all, seen


def columns_of(ref, rows, part=slice(None)):
    return jnp.concatenate([ref[part, at] for at in rows], axis=1)


def hidden(scores, block, places):
    k_places = block * KEYS + lax.broadcasted_iota(jnp.int32, (KEYS, TILE), 0)
    return jnp.where(k_places <= places, scores, masked_score)


def forward_kernel(
    heads, groups, runs, q_runs_ref, q_order_ref, k_runs_ref, q_ref, o_grad_ref, *refs
):
    kv_refs = refs[:groups]
    out_ref, kv, kv_turned, log_ref, delta_ref, first_w, state, out_total = refs[groups:]
    pair = 2 * HD

    for source in range(groups):

        def place(run, carry, source=source):
            at = pl.multiple_of(k_runs_ref[source * runs + run] * RUN, RUN)
            columns = kv_refs[source][:, pl.ds(pl.multiple_of(run * RUN, RUN), RUN)]
            kv_turned[:, pl.ds(at, RUN)] = columns
            for head in range(heads):
                part = slice(head * pair, (head + 1) * pair)
                kv[pl.ds(at, RUN), part] = columns[part, :].T
            return carry

        lax.fori_loop(0, runs, place, 0)

    def tile_step(tile, carry):
        rows, places, seen_by_all, seen = tile_of(tile, q_runs_ref, q_order_ref)
        nothing = jnp.zeros((HD, TILE), low)
        for head in range(heads):
            part = slice(head * HD, (head + 1) * HD)
            first_w[head] = jnp.concatenate([columns_of(q_ref, rows, part), nothing], axis=0)
        state[...] = jnp.full(state.shape, masked_score, full)
        out_total[...] = jnp.zeros_like(out_total)

        def step(hides, block, sums):
            at = pl.ds(pl.multiple_of(block * KEYS, KEYS), KEYS)
            new_sums = []
            for head in range(heads):
                part = slice(head * pair, (head + 1) * pair)
                scores = dot(kv[at, part], first_w[head])
                if hides:
                    scores = hidden(scores, block, places)
                old_max = state[head : head + 1, :]
                new_max = jnp.maximum(old_max, jnp.max(scores, axis=0, keepdims=True))
                weights = jnp.exp(scores - new_max)
                fading = jnp.exp(old_max - new_max)
                state[head : head + 1, :] = new_max
                new_sums.append(sums[head] * fading + jnp.sum(weights, axis=0, keepdims=True))
                here = slice(head * HD, (head + 1) * HD)
                values = kv_turned[head * pair + HD : (head + 1) * pair, at]
                out_total[here, :] = out_total[here, :] * fading + dot(values, weights.astype(low))
            return tuple(new_sums)

        sums = tuple(jnp.zeros((1, TILE), full) for _ in range(heads))
        sums = lax.fori_loop(0, seen_by_all, functools.partial(step, False), sums)
        sums = lax.fori_loop(seen_by_all, seen, functools.partial(step, True), sums)
        for head in range(heads):
            here = slice(head * HD, (head + 1) * HD)
            attended = out_total[here, :] / sums[head]
            log_total = state[head : head + 1, :] + jnp.log(sums[head])
            o_grad = columns_of(o_grad_ref, rows, here).astype(full)
            delta = jnp.sum(o_grad * attended, axis=0, keepdims=True)
            for half, at in enumerate(rows):
                columns = slice(half * RUN, (half + 1) * RUN)
                out_ref[here, at] = attended[:, columns].astype(low)
                log_ref[head : head + 1, at] = log_total[:, columns]
                delta_ref[head : head + 1, at] = delta[:, columns]
        return carry

    lax.fori_loop(0, q_ref.shape[1] // TILE, tile_step, 0)


def backward_kernel(
    heads,
    groups,
    runs,
    q_runs_ref,
    q_order_ref,
    k_runs_ref,
    q_ref,
    o_grad_ref,
    kv,
    kv_turned,
    log_ref,
    delta_ref,
    q_grad_ref,
    *refs,
):
    kv_grad_refs = refs[:groups]
    total, first_w, second_w, q_total = refs[groups:]
    pair = 2 * HD
    total[...] = jnp.zeros_like(total)

    def tile_step(tile, carry):
        rows, places, seen_by_all, seen = tile_of(tile, q_runs_ref, q_order_ref)
        nothing = jnp.zeros((HD, TILE), low)
        for head in range(heads):
            part = slice(head * HD, (head + 1) * HD)
            upper = jnp.concatenate([columns_of(q_ref, rows, part), nothing], axis=0)
            lower = jnp.concatenate([nothing, columns_of(o_grad_ref, rows, part)], axis=0)
            first_w[head, :, :TILE] = upper
            first_w[head, :, TILE:] = lower
            second_w[head, :TILE, :] = upper.T
            second_w[head, TILE:, :] = lower.T
        q_total[...] = jnp.zeros_like(q_total)
        log_totals = columns_of(log_ref, rows)
        deltas = columns_of(delta_ref, rows)

        def step(hides, block, carry):
            at = pl.ds(pl.multiple_of(block * KEYS, KEYS), KEYS)
            for head in range(heads):
                part = slice(head * pair, (head + 1) * pair)
                both = dot(kv[at, part], first_w[head])
                scores = both[:, :TILE]
                if hides:
                    scores = hidden(scores, block, places)
                chances = jnp.exp(scores - log_totals[head : head + 1, :])
                score_grad = chances * (both[:, TILE:] - deltas[head : head + 1, :])
                score_grad = score_grad.astype(low)
                joint = jnp.concatenate([score_grad, chances.astype(low)], axis=1)
                total[at, part] += dot(joint, second_w[head])
                here = slice(head * HD, (head + 1) * HD)
                keys = kv_turned[head * pair : head * pair + HD, at]
                q_total[here, :] += dot(keys, score_grad)
            return carry

        lax.fori_loop(0, seen_by_all, functools.partial(step, False), 0)
        lax.fori_loop(seen_by_all, seen, functools.partial(step, True), 0)
        for half, at in enumerate(rows):
            q_grad_ref[:, at] = q_total[:, half * RUN : (half + 1) * RUN]
        return carry

    lax.fori_loop(0, q_ref.shape[1] // TILE, tile_step, 0)

    for source in range(groups):

        def give(run, carry, source=source):
            at = pl.multiple_of(k_runs_ref[source * runs + run] * RUN, RUN)
            columns = pl.ds(pl.multiple_of(run * RUN, RUN), RUN)
            rows = total[pl.ds(at, RUN), :].astype(low)
            for head in range(heads):
                part = slice(head * pair, (head + 1) * pair)
                kv_grad_refs[source][part, columns] = rows[:, part].T
            return carry

        lax.fori_loop(0, runs, give, 0)


def attention_call(kernel, name, tables, operands, out_shape, scratch, groups, work):
    width, count = operands[0].shape
    heads, runs = width // HD, count // RUN
    pairs = count * groups * count * heads // 2
    smem = pl.BlockSpec(memory_space=pltpu.SMEM)
    vmem = pl.BlockSpec(memory_space=pltpu.VMEM)
    return pl.pallas_call(
        functools.partial(kernel, heads, groups, runs),
        out_shape=out_shape,
        in_specs=[smem] * len(tables) + [vmem] * len(operands),
        out_specs=tuple([vmem] * len(out_shape)),
        scratch_shapes=scratch,
        compiler_params=pltpu.CompilerParams(vmem_limit_bytes=(16 + 5 * groups) * 2**20),
        cost_estimate=pl.CostEstimate(
            flops=work * pairs,
            bytes_accessed=8 * count * width * groups,
            transcendentals=pairs,
        ),
        name=name,
    )(*tables, *operands)


def attend(tables, queries, o_grads, kv_parts):
    width, count = queries.shape
    keys = len(kv_parts) * count
    out_shape = (
        jax.ShapeDtypeStruct((width, count), low),
        jax.ShapeDtypeStruct((keys, 2 * width), low),
        jax.ShapeDtypeStruct((2 * width, keys), low),
        jax.ShapeDtypeStruct((8, count), full),
        jax.ShapeDtypeStruct((8, count), full),
    )
    scratch = [
        pltpu.VMEM((width // HD, 2 * HD, TILE), low),
        pltpu.VMEM((8, TILE), full),
        pltpu.VMEM((width, TILE), full),
    ]
    operands = (queries, o_grads) + tuple(kv_parts)
    groups = len(kv_parts)
    return attention_call(
        forward_kernel, "attend", tables, operands, out_shape, scratch, groups, 6000
    )


def attend_back(tables, queries, o_grads, kv, kv_turned, log_totals, deltas):
    width, count = queries.shape
    keys = kv.shape[0]
    groups = keys // count
    out_shape = (jax.ShapeDtypeStruct((width, count), full),) + (
        jax.ShapeDtypeStruct((2 * width, count), low),
    ) * groups
    scratch = [
        pltpu.VMEM((keys, 2 * width), full),
        pltpu.VMEM((width // HD, 2 * HD, 2 * TILE), low),
        pltpu.VMEM((width // HD, 2 * TILE, 2 * HD), low),
        pltpu.VMEM((width, TILE), full),
    ]
    operands = (queries, o_grads, kv, kv_turned, log_totals, deltas)
    out = attention_call(
        backward_kernel, "attend_back", tables, operands, out_shape, scratch, groups, 6000
    )
    return out[0], out[1:]


def prepare_kernel(heads, order_ref, source_ref, cosine_ref, sine_ref, *refs):
    x_refs, piece_refs, outs = refs[:TP], refs[TP:-6], refs[-6:]
    q_ref, kv_ref, first_ref, second_ref, matrix_ref, small_ref = outs
    span = heads * HD
    block, width = x_refs[0].shape
    rows = jnp.concatenate([piece[...] for piece in piece_refs], axis=0)
    columns = dot(order_ref[...], rows).astype(low)
    turned_columns = columns.T
    matrix = turned_columns[: 3 * span]
    small = turned_columns[3 * span :].astype(full)
    matrix_ref[...] = matrix
    small_ref[...] = small
    gain_one, shift_one, gain_two, shift_two = (small[k : k + 1] for k in range(4))

    shift = jnp.zeros((3 * span, 1), full)
    lane = lax.broadcasted_iota(jnp.int32, (3 * span, HD), 1)
    feature = lax.broadcasted_iota(jnp.int32, (3 * span, width), 1)
    for k in range(3):
        chosen = (source_ref[...] == 3 * feature + k).astype(full).astype(low)
        found = dot(chosen, columns[:, 3 * span :])
        shift += jnp.sum(jnp.where(lane == 6 + k, found, 0.0), axis=1, keepdims=True)

    cosines, sines = cosine_ref[...], sine_ref[...]
    half_dims = ROT // 2

    def rotated(head, at):
        cosine, sine = cosines[:, at], sines[:, at]
        first, second = head[:half_dims], head[half_dims:ROT]
        return jnp.concatenate(
            [first * cosine - second * sine, second * cosine + first * sine, head[ROT:]], axis=0
        )

    for piece in range(TP):
        at = slice(piece * block, (piece + 1) * block)
        x = x_refs[piece][...].astype(full)
        centred = x - jnp.mean(x, axis=1, keepdims=True)
        spread = jnp.mean(centred * centred, axis=1, keepdims=True)
        normed = centred * lax.rsqrt(spread + norm_eps)
        first_low = (normed * gain_one + shift_one).astype(low)
        first_ref[at, :] = first_low
        second_ref[at, :] = (normed * gain_two + shift_two).astype(low)
        joined = dot(matrix, first_low, ((1,), (1,))) + shift
        for head in range(heads):
            here = slice(head * HD, (head + 1) * HD)
            queries = rotated(joined[here], at).astype(low)
            q_ref[here, at] = queries * jnp.asarray(HD**-0.5, low)
            to_key = span + 2 * head * HD
            to_value = to_key + HD
            kv_ref[2 * head * HD : (2 * head + 1) * HD, at] = rotated(
                joined[to_key:to_value], at
            ).astype(low)
            kv_ref[(2 * head + 1) * HD : (2 * head + 2) * HD, at] = joined[
                to_value : to_value + HD
            ].astype(low)


def prepare(heads, order, source, cosines, sines, x_pieces, row_pieces):
    block, width = x_pieces[0].shape
    count, span = TP * block, heads * HD
    return pl.pallas_call(
        functools.partial(prepare_kernel, heads),
        out_shape=(
            jax.ShapeDtypeStruct((span, count), low),
            jax.ShapeDtypeStruct((2 * span, count), low),
            jax.ShapeDtypeStruct((count, width), low),
            jax.ShapeDtypeStruct((count, width), low),
            jax.ShapeDtypeStruct((3 * span, width), low),
            jax.ShapeDtypeStruct((HD, width), full),
        ),
        compiler_params=pltpu.CompilerParams(vmem_limit_bytes=40 * 2**20),
        cost_estimate=pl.CostEstimate(
            flops=50 * width * span * count, bytes_accessed=16 * count * width, transcendentals=count
        ),
        name="prepare",
    )(order, source, cosines, sines, *x_pieces, *row_pieces)


def finish_kernel(
    heads,
    order_ref,
    place_ref,
    source_ref,
    cosine_ref,
    sine_ref,
    matrix_ref,
    gain_ref,
    early_ref,
    q_grad_ref,
    first_ref,
    slope_in_ref,
    merge_ref,
    *refs,
):
    x_refs, kv_refs, outs = refs[:TP], refs[TP:-4], refs[-4:]
    rows_ref, slope_ref, gradient, joined = outs
    span = heads * HD
    block, width = x_refs[0].shape
    half_dims = ROT // 2
    cosine, sine = cosine_ref[...], sine_ref[...]

    def rotated_back(head):
        first, second = head[:half_dims], head[half_dims:ROT]
        return jnp.concatenate(
            [first * cosine + second * sine, second * cosine - first * sine, head[ROT:]], axis=0
        )

    for head in range(heads):
        here = slice(head * HD, (head + 1) * HD)
        joined[here, :] = rotated_back(q_grad_ref[here, :] * HD**-0.5).astype(low)
        key = slice(2 * head * HD, (2 * head + 1) * HD)
        value = slice((2 * head + 1) * HD, (2 * head + 2) * HD)
        key_grad, value_grad = (
            functools.reduce(jnp.add, [ref[part, :].astype(full) for ref in kv_refs])
            for part in (key, value)
        )
        to_key = span + 2 * head * HD
        joined[to_key : to_key + HD, :] = rotated_back(key_grad).astype(low)
        joined[to_key + HD : to_key + 2 * HD, :] = value_grad.astype(low)

    gain_sum, shift_sum = jnp.zeros((1, width), full), jnp.zeros((1, width), full)
    gain = gain_ref[...]
    for piece in range(TP):
        at = slice(piece * block, (piece + 1) * block)
        x = x_refs[piece][...].astype(full)
        centred = x - jnp.mean(x, axis=1, keepdims=True)
        spread = jnp.mean(centred * centred, axis=1, keepdims=True)
        normed = centred * lax.rsqrt(spread + norm_eps)
        first_gradient = dot(joined[:, at].T, matrix_ref[...])
        gain_sum += jnp.sum(first_gradient * normed, axis=0, keepdims=True)
        shift_sum += jnp.sum(first_gradient, axis=0, keepdims=True)
        slope_ref[at, :] = (first_gradient * gain + slope_in_ref[at, :]).astype(low)

    gradient[...] = dot(joined[...], first_ref[...]).astype(low)
    order = order_ref[...]
    rows_ref[:, : 3 * span] = dot(order, gradient[...], ((1,), (1,))).astype(low)
    sums = jnp.concatenate(
        [gain_sum, shift_sum, early_ref[2:, :], jnp.zeros((HD - early_ref.shape[0], width), full)],
        axis=0,
    )
    sums = dot(order, sums.astype(low), ((1,), (1,)))
    joined_sum = jnp.sum(joined[...].astype(full), axis=1, keepdims=True)
    joined_sum = jnp.broadcast_to(joined_sum, (3 * span, HD)).astype(low)
    lane = lax.broadcasted_iota(jnp.int32, (width, HD), 1)
    for k in range(3):
        chosen = (source_ref[...] == 3 * place_ref[...] + k).astype(full).astype(low)
        sums = jnp.where(lane == 5 + k, dot(chosen, joined_sum), sums)
    rows_ref[:, 3 * span : 3 * span + HD] = sums.astype(low)
    rows_ref[:, 3 * span + HD :] = merge_ref[...]


def finish(
    heads,
    order,
    place,
    source,
    cosines,
    sines,
    matrix,
    gain,
    early,
    q_grad,
    first_low,
    slope,
    merge_rows,
    x_pieces,
    kv_grads,
):
    block, width = x_pieces[0].shape
    count, span = TP * block, heads * HD
    return pl.pallas_call(
        functools.partial(finish_kernel, heads),
        out_shape=(
            jax.ShapeDtypeStruct((width, 3 * span + HD + width), low),
            jax.ShapeDtypeStruct((count, width), low),
        ),
        scratch_shapes=[pltpu.VMEM((3 * span, width), low), pltpu.VMEM((3 * span, count), low)],
        compiler_params=pltpu.CompilerParams(vmem_limit_bytes=40 * 2**20),
        cost_estimate=pl.CostEstimate(
            flops=50 * width * span * count, bytes_accessed=16 * count * width, transcendentals=count
        ),
        name="finish",
    )(
        order,
        place,
        source,
        cosines,
        sines,
        matrix,
        gain,
        early,
        q_grad,
        first_low,
        slope,
        merge_rows,
        *x_pieces,
        *kv_grads,
    )


def on_device(
    tokens,
    positions,
    gain_attention,
    bias_attention,
    gain_feed,
    bias_feed,
    weight_joined,
    bias_joined,
    weight_merge,
    bias_merge,
    weight_expand,
    bias_expand,
    weight_reduce,
    bias_reduce,
    cotangent,
):
    seqs, block, width = tokens.shape
    units = weight_expand.shape[1]
    copies = lax.axis_size("dp")
    members = lax.axis_size("blk")
    groups = members // TP
    here = lax.axis_index("blk")
    my_part, my_group, my_copy = here // groups, here % groups, lax.axis_index("dp")
    heads = width // HD // TP
    depth = weight_joined.shape[0]
    part_units = units // TP
    my_units = weight_reduce.shape[0]
    span = heads * HD

    def over_parts(value, away):
        return lax.ppermute(value, "blk", [(i, i ^ (away * groups)) for i in range(members)])

    def over_groups(value, away):
        return lax.ppermute(value, "blk", [(i, i ^ away) for i in range(members)])

    def over_copies(value, away):
        return lax.ppermute(value, "dp", [(i, i ^ away) for i in range(copies)])

    part_lines = [[part * groups + g for part in range(TP)] for g in range(groups)]
    group_planes = [[part * groups + g for g in range(groups)] for part in range(TP)]

    def swapped(value, lines):
        return lax.all_to_all(value, "blk", 0, 0, axis_index_groups=lines, tiled=True)

    def from_mine(value, me, axis):
        count = value.shape[axis]
        bit = 1
        while bit < count:
            split = value.reshape(value.shape[:axis] + (-1, 2, bit) + value.shape[axis + 1 :])
            flipped = jnp.flip(split, axis + 1).reshape(value.shape)
            value = jnp.where(me // bit % 2 == 1, flipped, value)
            bit *= 2
        return value

    def picked(value, at, axis):
        return lax.dynamic_index_in_dim(value, at, axis, keepdims=False)

    def exchanged(value, move, count, me, axis):
        return [picked(value, me, axis)] + [
            move(picked(value, me ^ away, axis), away) for away in range(1, count)
        ]

    def halved(value, move, count, me):
        while count > 1:
            count //= 2
            halves = value.reshape((2, count) + value.shape[1:])
            upper = me // count % 2
            sent = move(picked(halves, 1 - upper, 0).astype(low), count)
            value = picked(halves, upper, 0).astype(full) + sent.astype(full)
        return value[0]

    def ready(value):
        first = value[(0,) * value.ndim]
        return first == first

    def added(pieces):
        return functools.reduce(jnp.add, [piece.astype(full) for piece in pieces])

    def placed(pieces, me):
        out = jnp.zeros((len(pieces),) + pieces[0].shape, pieces[0].dtype)
        for away, piece in enumerate(pieces):
            out = lax.dynamic_update_index_in_dim(out, piece, me ^ away, 0)
        return out

    def of_group(value):
        return jnp.concatenate([value] + [over_parts(value, away) for away in range(1, TP)], axis=0)

    count = TP * block
    runs = count // RUN

    def as_columns(vector):
        return vector.reshape(depth, -1)

    starts = (positions.reshape(-1)[::RUN] // RUN).astype(low)
    starts = jnp.pad(starts, (0, depth - starts.shape[0]))
    small = jnp.concatenate(
        [
            as_columns(vector)
            for vector in (
                gain_attention,
                bias_attention,
                gain_feed,
                bias_feed,
                bias_merge,
                bias_reduce,
                bias_joined,
                bias_expand,
                starts,
            )
        ],
        axis=1,
    )
    small = jnp.pad(small, ((0, 0), (0, HD - small.shape[1])))

    def by_head(matrix):
        lead = matrix.shape[:-1]
        split = matrix.reshape(lead + (3, TP, heads, HD))
        queries = split[..., 0, :, :, :].reshape(lead + (TP, span))
        kv = jnp.stack([split[..., 1, :, :, :], split[..., 2, :, :, :]], axis=-2)
        return jnp.concatenate([queries, kv.reshape(lead + (TP, 2 * span))], axis=-1)

    def from_head(matrix):
        lead = matrix.shape[:-2]
        queries = matrix[..., :span].reshape(lead + (1, TP, heads, HD))
        kv = matrix[..., span:].reshape(lead + (TP, heads, 2, HD))
        kv = jnp.moveaxis(kv, -2, len(lead))
        return jnp.concatenate([queries, kv], axis=len(lead)).reshape(lead + (3 * width,))

    expand_parts = weight_expand.reshape(depth, copies, TP, groups * my_units)
    expand_parts = jnp.moveaxis(expand_parts, 2, 0).reshape(TP, depth, part_units)
    parts = jnp.concatenate(
        [
            expand_parts,
            jnp.broadcast_to(weight_merge, (TP, depth, width)),
            jnp.swapaxes(by_head(weight_joined), 0, 1),
            jnp.broadcast_to(small, (TP, depth, HD)),
        ],
        axis=2,
    )
    tokens = jnp.where(ready(parts), tokens, jnp.zeros_like(tokens))
    to_merge, to_joined = part_units, part_units + width
    to_small = 3 * span
    mine = swapped(parts, part_lines).reshape(my_units, -1)
    own_low = tokens.reshape(block, width)
    own_later = jnp.where(ready(mine), own_low, jnp.zeros_like(own_low))
    x_pieces = [own_low, over_parts(own_low, 1)]
    x_pieces += [over_parts(own_later, away) for away in range(2, TP)]
    rows = own_low.astype(full)
    first_rows = mine[:, to_joined:]
    mine = jnp.concatenate([mine[:, :to_joined], weight_reduce], axis=1)
    def in_plane(value):
        value = swapped(jnp.broadcast_to(value, (groups,) + value.shape), group_planes)
        return value.reshape(groups * my_units, -1)

    def of_copies(value):
        return [value] + [over_copies(value, away) for away in range(1, copies)]

    near = in_plane(first_rows)
    row_pieces = of_copies(near)
    all_rows = jnp.concatenate(of_copies(in_plane(mine)), axis=0)
    upstream_sent, *_ = lax.optimization_barrier((cotangent, *x_pieces[1:]))
    came = jnp.arange(width, dtype=jnp.int32)
    row, came_part = came % depth, (came // depth) % TP
    came_group = (came // (depth * TP)) % groups
    came_copy = came // (depth * TP * groups) ^ my_copy
    place_of = ((came_copy * TP + came_part) * groups + came_group) * depth + row
    wanted = jnp.arange(width, dtype=jnp.int32)[:, None]
    order = (place_of[None, :] == wanted).astype(low)
    back_order = (place_of[:, None] == wanted[:, 0]).astype(low)
    source = jnp.arange(3 * width, dtype=jnp.int32)
    unit = jnp.arange(part_units, dtype=jnp.int32)
    unit_group = (unit // my_units) % groups
    unit_copy = unit // (my_units * groups) ^ my_copy
    unit_place = (unit_copy * groups + unit_group) * my_units + unit % my_units
    unit_order = (unit_place[None, :] == unit[:, None]).astype(low)

    def ordered(matrix_order, columns):
        return dot(matrix_order, columns).astype(low)

    expand_matrix = ordered(order, all_rows[:, :to_merge])
    head_order = lax.dynamic_slice_in_dim(order, my_part * span, span, 0)
    merge_matrix = ordered(head_order, all_rows[:, to_merge:to_joined])
    reduce_matrix = ordered(unit_order, all_rows[:, to_joined:])

    run_starts = near[:, to_small + 13].reshape(groups, TP, depth)
    run_starts = from_mine(from_mine(run_starts, my_group, 0), my_part, 1)
    k_runs = run_starts[:, :, : block // RUN].astype(jnp.int32).reshape(groups, runs)
    q_runs = k_runs[0]
    places = (q_runs[:, None] * RUN + jnp.arange(RUN, dtype=jnp.int32)).reshape(count)

    half_dims = ROT // 2
    frequency = jnp.exp(jnp.arange(half_dims, dtype=full) * (-2.0 * math.log(10000.0) / ROT))
    angles = frequency[:, None] * places.astype(full)
    cosines, sines = jnp.cos(angles), jnp.sin(angles)
    my_source = picked(by_head(source), my_part, 0)
    queries, kv, first_low, second_low, joined_matrix, small_all = prepare(
        heads, order, my_source[:, None], cosines, sines, x_pieces, row_pieces
    )
    gain_one, _, gain_two, _, merge_shift, reduce_shift = small_all[:6]
    expand_shift = jnp.swapaxes(small_all[9:13], 0, 1)
    expand_shift = picked(expand_shift.reshape(copies, TP, groups * my_units), my_part, 1)
    expand_shift = expand_shift.reshape(-1)
    rank = jnp.sum(q_runs[None, :] < q_runs[:, None], axis=1)
    index = jnp.arange(runs, dtype=jnp.int32)
    q_order = jnp.sum(jnp.where(rank[None, :] == index[:, None], index[None, :], 0), axis=1)
    kv_parts = [kv] + [over_groups(kv, away) for away in range(1, groups)]

    upstream_low = of_group(upstream_sent.reshape(block, width))
    attended_gradient = dot(merge_matrix, upstream_low, ((1,), (1,))).astype(low)

    tables = (q_runs, q_order.astype(jnp.int32), k_runs.reshape(-1))
    attended_low, kv_sorted, kv_turned, log_totals, deltas = attend(
        tables, queries, attended_gradient, kv_parts
    )
    query_total, kv_totals = attend_back(
        tables, queries, attended_gradient, kv_sorted, kv_turned, log_totals, deltas
    )

    expanded = dot(second_low, expand_matrix) + expand_shift
    active, gelu_pull = jax.vjp(lambda v: jax.nn.gelu(v, approximate=False), expanded)
    active_low = active.astype(low)
    active_gradient = dot(upstream_low, reduce_matrix, ((1,), (1,)))
    expanded_gradient = gelu_pull(active_gradient)[0].astype(low)
    second_gradient = dot(expanded_gradient, expand_matrix, ((1,), (1,)))

    def of_rows(partial):
        chunks = partial.astype(low).reshape(TP, block, width)
        mine = partial.reshape(TP, block, width)[0]
        return added([mine] + [over_parts(chunks[away], away) for away in range(1, TP)])

    middle = jnp.mean(rows, axis=-1, keepdims=True)
    centred = rows - middle
    inverse = lax.rsqrt(jnp.mean(centred * centred, axis=-1, keepdims=True) + norm_eps)
    own = centred * inverse

    branches = of_rows(
        dot(active_low, reduce_matrix) + dot(attended_low, merge_matrix, ((0,), (0,)))
    )
    result = (rows + branches + merge_shift + reduce_shift).astype(low)

    def by_rows(matrix):
        matrix = jnp.swapaxes(matrix.reshape(copies, TP, groups, depth, -1), 1, 2)
        return matrix.reshape(copies, groups, my_units, -1)

    def sent_halves(value, move, count):
        while count > 1:
            count //= 2
            value = value.reshape((2, -1) + value.shape[1:])
            value = value[0].astype(full) + move(value[1].astype(low), count).astype(full)
        return value

    expand_rows = dot(second_low, expanded_gradient, ((0,), (0,))).astype(low)
    reduce_rows = dot(active_low, upstream_low, ((0,), (0,))).astype(low)
    reduce_rows = reduce_rows.reshape(copies, groups, my_units, width)
    later = halved(
        jnp.concatenate([by_rows(expand_rows), reduce_rows], axis=-1), over_copies, copies, my_copy
    )
    later = swapped(later.astype(low), group_planes)
    later, attended_then, kv_totals, _, _ = lax.optimization_barrier(
        (later, attended_low, kv_totals, query_total, result)
    )
    later = jnp.sum(later.astype(full), axis=0)
    gradient_weight_reduce = later[:, part_units:]
    merge_rows = dot(attended_then, upstream_low).astype(low)
    merge_rows = dot(head_order, merge_rows, ((0,), (0,))).astype(low)
    later = later[:, :part_units].astype(low)

    upstream = cotangent.reshape(block, width).astype(full)
    x_low = jnp.concatenate(x_pieces, axis=0).astype(full)
    x_centred = x_low - jnp.mean(x_low, axis=-1, keepdims=True)
    x_inverse = lax.rsqrt(jnp.mean(x_centred * x_centred, axis=-1, keepdims=True) + norm_eps)
    expand_sum = jnp.sum(expanded_gradient.astype(full), axis=0).reshape(copies, -1)
    expand_sum = jnp.swapaxes(placed_alone(expand_sum, my_part, TP), 0, 1).reshape(width, -1)
    nothing = jnp.zeros((width,), full)
    early = jnp.stack(
        [
            nothing,
            nothing,
            jnp.sum(second_gradient * x_centred * x_inverse, axis=0),
            jnp.sum(second_gradient, axis=0),
            jnp.sum(upstream, axis=0),
            nothing,
            nothing,
            nothing,
        ]
    )
    early = jnp.concatenate([early, expand_sum.T], axis=0)
    kv_grads = [kv_totals[0]] + [over_groups(kv_totals[r], r) for r in range(1, groups)]
    final, slope = finish(
        heads,
        back_order,
        place_of[:, None],
        my_source[None, :],
        cosines,
        sines,
        joined_matrix,
        gain_one[None, :],
        early,
        query_total,
        first_low,
        second_gradient * gain_two,
        merge_rows,
        x_pieces,
        kv_grads,
    )
    slope = of_rows(slope)
    gradient_tokens = upstream + inverse * (
        slope
        - jnp.mean(slope, axis=-1, keepdims=True)
        - own * jnp.mean(slope * own, axis=-1, keepdims=True)
    )

    final = sent_halves(final, over_copies, copies).astype(low)
    final = swapped(final.reshape(groups, my_units, -1), group_planes)
    final = jnp.concatenate([jnp.sum(final.astype(full), axis=0).astype(low), later], axis=1)
    final = swapped(final.reshape(TP, depth, -1), part_lines)
    to_rest = 3 * span + HD
    gradient_weight_joined = from_head(jnp.swapaxes(final[..., : 3 * span], 0, 1))
    small_total = jnp.sum(final[..., 3 * span : to_rest].astype(full), axis=0)
    gradient_weight_merge = jnp.sum(final[..., to_rest : to_rest + width].astype(full), axis=0)
    gradient_weight_expand = final[..., to_rest + width :]
    gradient_weight_expand = jnp.moveaxis(
        gradient_weight_expand.reshape(TP, depth, copies, groups * my_units), 0, 2
    ).reshape(depth, units)
    gradients = small_total[:, :5].T
    gradient_bias_joined = small_total[:, 5:8].reshape(-1)
    gradient_bias_expand = small_total[:, 8:12].reshape(-1)

    def wide(value):
        return value.astype(full)

    return (
        result.reshape(tokens.shape),
        gradient_tokens.reshape(tokens.shape),
        gradients[0],
        gradients[1],
        gradients[2],
        gradients[3],
        wide(gradient_weight_joined),
        gradient_bias_joined,
        wide(gradient_weight_merge),
        gradients[4],
        wide(gradient_weight_expand),
        gradient_bias_expand,
        wide(gradient_weight_reduce),
        gradients[4],
    )


def placed_alone(value, at, count):
    out = jnp.zeros((count,) + value.shape, value.dtype)
    return lax.dynamic_update_index_in_dim(out, value, at, 0)


def solution(mesh):
    rows = P("dp", "blk", None)
    vector, matrix = P(("dp", "blk")), P(("dp", "blk"), None)
    params = (vector,) * 4 + (matrix, vector) * 4
    return jax.shard_map(
        on_device,
        mesh=mesh,
        in_specs=(rows, P("dp", "blk")) + params + (rows,),
        out_specs=(rows, rows) + params,
        check_vma=False,
    )
```

```python
import functools
import math

import jax
import jax.numpy as jnp
from jax import lax
from jax.experimental import pallas as pl
from jax.experimental.pallas import tpu as pltpu
from jax.sharding import PartitionSpec as P

HD = 64
ROT = 16
TP = 4
RUN = 128
TILE = 2 * RUN
FORWARD_KEYS, FORWARD_REST = 1024, 1024
BACKWARD_KEYS, BACKWARD_REST = 1024, 512
VMEM = 56 * 2**20

norm_eps = 1e-05
masked_score = -1e30
low = jnp.bfloat16
full = jnp.float32


def dot(a, b, dims=((1,), (0,))):
    return lax.dot_general(a, b, (dims, ((), ())), preferred_element_type=full)


def tile_of(tile, q_runs_ref, q_order_ref):
    early, late = q_order_ref[2 * tile], q_order_ref[2 * tile + 1]
    early_run, late_run = q_runs_ref[early], q_runs_ref[late]
    rows = [pl.ds(pl.multiple_of(run * RUN, RUN), RUN) for run in (early, late)]
    column = lax.broadcasted_iota(jnp.int32, (1, TILE), 1)
    places = jnp.where(column < RUN, early_run * RUN + column, late_run * RUN + column - RUN)
    return rows, places, early_run * RUN, late_run * RUN + RUN


def over_keys(step, by_all, by_some, many, few, carry):
    blocks = lax.div(by_all, many)
    carry = lax.fori_loop(0, blocks, functools.partial(step, False, many), carry)
    first = blocks * (many // few)
    last = lax.div(by_some + few - 1, few)
    return lax.fori_loop(first, last, functools.partial(step, True, few), carry)


def columns_of(ref, rows, part=slice(None)):
    return jnp.concatenate([ref[part, at] for at in rows], axis=1)


def hidden(scores, first, places):
    k_places = first + lax.broadcasted_iota(jnp.int32, scores.shape, 0)
    return jnp.where(k_places <= places, scores, masked_score)


def forward_kernel(
    heads, groups, runs, q_runs_ref, q_order_ref, k_runs_ref, q_ref, o_grad_ref, *refs
):
    merge_ref, fed_ref, *kv_refs = refs[: groups + 2]
    out_ref, kv, kv_turned, log_ref, delta_ref, *branch_refs = refs[groups + 2 : -3]
    first_w, state, out_total = refs[-3:]
    pair = 2 * HD

    for source in range(groups):

        def place(run, carry, source=source):
            at = pl.multiple_of(k_runs_ref[source * runs + run] * RUN, RUN)
            columns = kv_refs[source][:, pl.ds(pl.multiple_of(run * RUN, RUN), RUN)]
            kv_turned[:, pl.ds(at, RUN)] = columns
            for head in range(heads):
                part = slice(head * pair, (head + 1) * pair)
                kv[pl.ds(at, RUN), part] = columns[part, :].T
            return carry

        lax.fori_loop(0, runs, place, 0)

    def tile_step(tile, carry):
        rows, places, by_all, by_some = tile_of(tile, q_runs_ref, q_order_ref)
        nothing = jnp.zeros((HD, TILE), low)
        for head in range(heads):
            part = slice(head * HD, (head + 1) * HD)
            first_w[head] = jnp.concatenate([columns_of(q_ref, rows, part), nothing], axis=0)
        state[...] = jnp.full(state.shape, masked_score, full)
        out_total[...] = jnp.zeros_like(out_total)

        def step(hides, size, block, sums):
            at = pl.ds(pl.multiple_of(block * size, size), size)
            new_sums = []
            products = [
                dot(kv[at, head * pair : (head + 1) * pair], first_w[head]) for head in range(heads)
            ]
            for head in range(heads):
                scores = products[head]
                if hides:
                    scores = hidden(scores, block * size, places)
                old_max = state[head : head + 1, :]
                new_max = jnp.maximum(old_max, jnp.max(scores, axis=0, keepdims=True))
                weights = jnp.exp(scores - new_max)
                fading = jnp.exp(old_max - new_max)
                state[head : head + 1, :] = new_max
                new_sums.append(sums[head] * fading + jnp.sum(weights, axis=0, keepdims=True))
                here = slice(head * HD, (head + 1) * HD)
                values = kv_turned[head * pair + HD : (head + 1) * pair, at]
                out_total[here, :] = out_total[here, :] * fading + dot(values, weights.astype(low))
            return tuple(new_sums)

        sums = tuple(jnp.zeros((1, TILE), full) for _ in range(heads))
        sums = over_keys(step, by_all, by_some, FORWARD_KEYS, FORWARD_REST, sums)
        for head in range(heads):
            here = slice(head * HD, (head + 1) * HD)
            attended = out_total[here, :] / sums[head]
            log_total = state[head : head + 1, :] + jnp.log(sums[head])
            o_grad = columns_of(o_grad_ref, rows, here).astype(full)
            delta = jnp.sum(o_grad * attended, axis=0, keepdims=True)
            for half, at in enumerate(rows):
                columns = slice(half * RUN, (half + 1) * RUN)
                out_ref[here, at] = attended[:, columns].astype(low)
                log_ref[head : head + 1, at] = log_total[:, columns]
                delta_ref[head : head + 1, at] = delta[:, columns]
        return carry

    lax.fori_loop(0, q_ref.shape[1] // TILE, tile_step, 0)

    block = branch_refs[0].shape[0]
    for piece, ref in enumerate(branch_refs):
        at = slice(piece * block, (piece + 1) * block)
        branch = dot(out_ref[:, at].T, merge_ref[...]) + fed_ref[at, :]
        ref[...] = branch.astype(ref.dtype)


def backward_kernel(
    heads,
    groups,
    runs,
    q_runs_ref,
    q_order_ref,
    k_runs_ref,
    q_ref,
    o_grad_ref,
    kv,
    kv_turned,
    log_ref,
    delta_ref,
    q_grad_ref,
    *refs,
):
    kv_grad_refs = refs[:groups]
    total, first_w, second_w, q_total = refs[groups:]
    pair = 2 * HD
    total[...] = jnp.zeros_like(total)

    def tile_step(tile, carry):
        rows, places, by_all, by_some = tile_of(tile, q_runs_ref, q_order_ref)
        nothing = jnp.zeros((HD, TILE), low)
        for head in range(heads):
            part = slice(head * HD, (head + 1) * HD)
            upper = jnp.concatenate([columns_of(q_ref, rows, part), nothing], axis=0)
            lower = jnp.concatenate([nothing, columns_of(o_grad_ref, rows, part)], axis=0)
            first_w[head, :, :TILE] = upper
            first_w[head, :, TILE:] = lower
            second_w[head, :TILE, :] = upper.T
            second_w[head, TILE:, :] = lower.T
        q_total[...] = jnp.zeros_like(q_total)
        log_totals = columns_of(log_ref, rows)
        deltas = columns_of(delta_ref, rows)

        def step(hides, size, block, carry):
            at = pl.ds(pl.multiple_of(block * size, size), size)
            products = [
                dot(kv[at, head * pair : (head + 1) * pair], first_w[head]) for head in range(heads)
            ]
            for head in range(heads):
                part = slice(head * pair, (head + 1) * pair)
                both = products[head]
                scores = both[:, :TILE]
                if hides:
                    scores = hidden(scores, block * size, places)
                chances = jnp.exp(scores - log_totals[head : head + 1, :])
                score_grad = chances * (both[:, TILE:] - deltas[head : head + 1, :])
                score_grad = score_grad.astype(low)
                joint = jnp.concatenate([score_grad, chances.astype(low)], axis=1)
                total[at, part] += dot(joint, second_w[head])
                here = slice(head * HD, (head + 1) * HD)
                keys = kv_turned[head * pair : head * pair + HD, at]
                q_total[here, :] += dot(keys, score_grad)
            return carry

        over_keys(step, by_all, by_some, BACKWARD_KEYS, BACKWARD_REST, 0)
        for half, at in enumerate(rows):
            q_grad_ref[:, at] = q_total[:, half * RUN : (half + 1) * RUN]
        return carry

    lax.fori_loop(0, q_ref.shape[1] // TILE, tile_step, 0)

    for source in range(groups):

        def give(run, carry, source=source):
            at = pl.multiple_of(k_runs_ref[source * runs + run] * RUN, RUN)
            columns = pl.ds(pl.multiple_of(run * RUN, RUN), RUN)
            rows = total[pl.ds(at, RUN), :].astype(low)
            for head in range(heads):
                part = slice(head * pair, (head + 1) * pair)
                kv_grad_refs[source][part, columns] = rows[:, part].T
            return carry

        lax.fori_loop(0, runs, give, 0)


def attention_call(kernel, name, tables, operands, out_shape, scratch, groups, work):
    width, count = operands[0].shape
    heads, runs = width // HD, count // RUN
    pairs = count * groups * count * heads // 2
    smem = pl.BlockSpec(memory_space=pltpu.SMEM)
    vmem = pl.BlockSpec(memory_space=pltpu.VMEM)
    return pl.pallas_call(
        functools.partial(kernel, heads, groups, runs),
        out_shape=out_shape,
        in_specs=[smem] * len(tables) + [vmem] * len(operands),
        out_specs=tuple([vmem] * len(out_shape)),
        scratch_shapes=scratch,
        compiler_params=pltpu.CompilerParams(vmem_limit_bytes=VMEM),
        cost_estimate=pl.CostEstimate(
            flops=work * pairs,
            bytes_accessed=8 * count * width * groups,
            transcendentals=pairs,
        ),
        name=name,
    )(*tables, *operands)


def pieces_of(block, width):
    kept = jax.ShapeDtypeStruct((block, width), full)
    return (kept,) + (jax.ShapeDtypeStruct((block, width), low),) * (TP - 1)


def attend(tables, queries, o_grads, merge_matrix, fed, kv_parts):
    width, count = queries.shape
    keys = len(kv_parts) * count
    out_shape = (
        jax.ShapeDtypeStruct((width, count), low),
        jax.ShapeDtypeStruct((keys, 2 * width), low),
        jax.ShapeDtypeStruct((2 * width, keys), low),
        jax.ShapeDtypeStruct((8, count), full),
        jax.ShapeDtypeStruct((8, count), full),
    ) + pieces_of(count // TP, fed.shape[1])
    scratch = [
        pltpu.VMEM((width // HD, 2 * HD, TILE), low),
        pltpu.VMEM((8, TILE), full),
        pltpu.VMEM((width, TILE), full),
    ]
    operands = (queries, o_grads, merge_matrix, fed) + tuple(kv_parts)
    groups = len(kv_parts)
    return attention_call(
        forward_kernel, "attend", tables, operands, out_shape, scratch, groups, 6000
    )


def attend_back(tables, queries, o_grads, kv, kv_turned, log_totals, deltas):
    width, count = queries.shape
    keys = kv.shape[0]
    groups = keys // count
    out_shape = (jax.ShapeDtypeStruct((width, count), full),) + (
        jax.ShapeDtypeStruct((2 * width, count), low),
    ) * groups
    scratch = [
        pltpu.VMEM((keys, 2 * width), full),
        pltpu.VMEM((width // HD, 2 * HD, 2 * TILE), low),
        pltpu.VMEM((width // HD, 2 * TILE, 2 * HD), low),
        pltpu.VMEM((width, TILE), full),
    ]
    operands = (queries, o_grads, kv, kv_turned, log_totals, deltas)
    out = attention_call(
        backward_kernel, "attend_back", tables, operands, out_shape, scratch, groups, 6000
    )
    return out[0], out[1:]


def prepare_kernel(heads, order_ref, source_ref, cosine_ref, sine_ref, *refs):
    x_refs, piece_refs, outs = refs[:TP], refs[TP:-6], refs[-6:]
    q_ref, kv_ref, first_ref, second_ref, matrix_ref, small_ref = outs
    span = heads * HD
    block, width = x_refs[0].shape
    rows = jnp.concatenate([piece[...] for piece in piece_refs], axis=0)
    columns = dot(order_ref[...], rows).astype(low)
    turned_columns = columns.T
    matrix = turned_columns[: 3 * span]
    small = turned_columns[3 * span :].astype(full)
    matrix_ref[...] = matrix
    small_ref[...] = small
    gain_one, shift_one, gain_two, shift_two = (small[k : k + 1] for k in range(4))

    shift = jnp.zeros((3 * span, 1), full)
    lane = lax.broadcasted_iota(jnp.int32, (3 * span, HD), 1)
    feature = lax.broadcasted_iota(jnp.int32, (3 * span, width), 1)
    for k in range(3):
        chosen = (source_ref[...] == 3 * feature + k).astype(full).astype(low)
        found = dot(chosen, columns[:, 3 * span :])
        shift += jnp.sum(jnp.where(lane == 6 + k, found, 0.0), axis=1, keepdims=True)

    cosines, sines = cosine_ref[...], sine_ref[...]
    half_dims = ROT // 2

    def rotated(head, at):
        cosine, sine = cosines[:, at], sines[:, at]
        first, second = head[:half_dims], head[half_dims:ROT]
        return jnp.concatenate(
            [first * cosine - second * sine, second * cosine + first * sine, head[ROT:]], axis=0
        )

    for piece in range(TP):
        at = slice(piece * block, (piece + 1) * block)
        x = x_refs[piece][...].astype(full)
        centred = x - jnp.mean(x, axis=1, keepdims=True)
        spread = jnp.mean(centred * centred, axis=1, keepdims=True)
        normed = centred * lax.rsqrt(spread + norm_eps)
        first_low = (normed * gain_one + shift_one).astype(low)
        first_ref[at, :] = first_low
        second_ref[at, :] = (normed * gain_two + shift_two).astype(low)
        joined = dot(matrix, first_low, ((1,), (1,))) + shift
        for head in range(heads):
            here = slice(head * HD, (head + 1) * HD)
            queries = rotated(joined[here], at).astype(low)
            q_ref[here, at] = queries * jnp.asarray(HD**-0.5, low)
            to_key = span + 2 * head * HD
            to_value = to_key + HD
            kv_ref[2 * head * HD : (2 * head + 1) * HD, at] = rotated(
                joined[to_key:to_value], at
            ).astype(low)
            kv_ref[(2 * head + 1) * HD : (2 * head + 2) * HD, at] = joined[
                to_value : to_value + HD
            ].astype(low)


def prepare(heads, order, source, cosines, sines, x_pieces, row_pieces):
    block, width = x_pieces[0].shape
    count, span = TP * block, heads * HD
    return pl.pallas_call(
        functools.partial(prepare_kernel, heads),
        out_shape=(
            jax.ShapeDtypeStruct((span, count), low),
            jax.ShapeDtypeStruct((2 * span, count), low),
            jax.ShapeDtypeStruct((count, width), low),
            jax.ShapeDtypeStruct((count, width), low),
            jax.ShapeDtypeStruct((3 * span, width), low),
            jax.ShapeDtypeStruct((HD, width), full),
        ),
        compiler_params=pltpu.CompilerParams(vmem_limit_bytes=VMEM),
        cost_estimate=pl.CostEstimate(
            flops=50 * width * span * count, bytes_accessed=16 * count * width, transcendentals=count
        ),
        name="prepare",
    )(order, source, cosines, sines, *x_pieces, *row_pieces)


def feed_kernel(
    heads,
    part_ref,
    order_ref,
    back_order_ref,
    unit_order_ref,
    unit_back_order_ref,
    gain_ref,
    shift_ref,
    second_ref,
    *refs,
):
    x_refs, up_refs, piece_refs, refs = refs[:TP], refs[TP : 2 * TP], refs[2 * TP : -11], refs[-11:]
    o_grad_ref, merge_ref, fed_ref, slope_ref, sums_ref, kept_ref, sent_ref = refs[:7]
    expand, reduce, active, gradient = refs[7:]
    span = heads * HD
    block, width = x_refs[0].shape
    units = expand.shape[1]
    rows = jnp.concatenate([piece[...] for piece in piece_refs], axis=0)
    expand[...] = dot(order_ref[...], rows[:, :units]).astype(low)
    reduce[...] = dot(unit_order_ref[...], rows[:, units + width :]).astype(low)
    mine = pl.ds(pl.multiple_of(part_ref[0] * span, span), span)
    merge_ref[...] = dot(order_ref[mine, :], rows[:, units : units + width]).astype(low)
    sums = [jnp.zeros((1, width), full)] * 2 + [jnp.zeros((1, units), full)]
    for piece in range(TP):
        at = slice(piece * block, (piece + 1) * block)
        up = up_refs[piece][...]
        expanded = dot(second_ref[at, :], expand[...]) + shift_ref[...]
        normal = 0.5 + 0.5 * lax.erf(expanded * 0.5**0.5)
        active_low = (expanded * normal).astype(low)
        active[at, :] = active_low
        fed_ref[at, :] = dot(active_low, reduce[...])
        o_grad_ref[:, at] = dot(merge_ref[...], up, ((1,), (1,))).astype(low)
        density = jnp.exp(-0.5 * expanded * expanded) * (2 * math.pi) ** -0.5
        expanded_gradient = dot(up, reduce[...], ((1,), (1,))) * (normal + expanded * density)
        gradient_low = expanded_gradient.astype(low)
        gradient[at, :] = gradient_low
        sums[2] += jnp.sum(gradient_low.astype(full), axis=0, keepdims=True)
        second_gradient = dot(gradient_low, expand[...], ((1,), (1,)))
        x = x_refs[piece][...].astype(full)
        centred = x - jnp.mean(x, axis=1, keepdims=True)
        spread = jnp.mean(centred * centred, axis=1, keepdims=True)
        normed = centred * lax.rsqrt(spread + norm_eps)
        sums[0] += jnp.sum(second_gradient * normed, axis=0, keepdims=True)
        sums[1] += jnp.sum(second_gradient, axis=0, keepdims=True)
        slope_ref[at, :] = second_gradient * gain_ref[...]
    sums_ref[...] = jnp.concatenate(sums + [jnp.zeros((5, width), full)], axis=0)
    up = jnp.concatenate([ref[...] for ref in up_refs], axis=0)
    expand_rows = dot(second_ref[...].T, gradient[...]).astype(low)
    reduce_rows = dot(active[...].T, up).astype(low)
    expand_rows = dot(back_order_ref[...], expand_rows).astype(low)
    reduce_rows = dot(unit_back_order_ref[...], reduce_rows).astype(low)
    half = width // 2
    for ref, at in ((kept_ref, slice(half)), (sent_ref, slice(half, width))):
        ref[:, :units] = expand_rows[at]
        ref[:, units:] = reduce_rows[at]


def feed(heads, part, orders, gain, shift, second_low, x_pieces, up_pieces, row_pieces):
    block, width = x_pieces[0].shape
    count, span, units = TP * block, heads * HD, shift.shape[1]
    rows_shape = jax.ShapeDtypeStruct((width // 2, units + width), low)
    operands = (*orders, gain, shift, second_low, *x_pieces, *up_pieces, *row_pieces)
    vmem = pl.BlockSpec(memory_space=pltpu.VMEM)
    return pl.pallas_call(
        functools.partial(feed_kernel, heads),
        out_shape=(
            jax.ShapeDtypeStruct((span, count), low),
            jax.ShapeDtypeStruct((span, width), low),
            jax.ShapeDtypeStruct((count, width), full),
            jax.ShapeDtypeStruct((count, width), full),
            jax.ShapeDtypeStruct((8, width), full),
            rows_shape,
            rows_shape,
        ),
        in_specs=[pl.BlockSpec(memory_space=pltpu.SMEM)] + [vmem] * len(operands),
        out_specs=(vmem,) * 7,
        scratch_shapes=[
            pltpu.VMEM((width, units), low),
            pltpu.VMEM((units, width), low),
            pltpu.VMEM((count, units), low),
            pltpu.VMEM((count, units), low),
        ],
        compiler_params=pltpu.CompilerParams(vmem_limit_bytes=VMEM),
        cost_estimate=pl.CostEstimate(flops=0, bytes_accessed=0, transcendentals=0),
        name="feed",
    )(part, *operands)


def finish_kernel(
    heads,
    part_ref,
    order_ref,
    place_ref,
    source_ref,
    cosine_ref,
    sine_ref,
    matrix_ref,
    gain_ref,
    early_ref,
    q_grad_ref,
    first_ref,
    slope_in_ref,
    merge_ref,
    *refs,
):
    x_refs, kv_refs, outs = refs[:TP], refs[TP:-5], refs[-5:]
    kept_ref, sent_ref, slope_ref, gradient, joined = outs
    span = heads * HD
    block, width = x_refs[0].shape
    half_dims = ROT // 2
    cosine, sine = cosine_ref[...], sine_ref[...]

    def rotated_back(head):
        first, second = head[:half_dims], head[half_dims:ROT]
        return jnp.concatenate(
            [first * cosine + second * sine, second * cosine - first * sine, head[ROT:]], axis=0
        )

    for head in range(heads):
        here = slice(head * HD, (head + 1) * HD)
        joined[here, :] = rotated_back(q_grad_ref[here, :] * HD**-0.5).astype(low)
        key = slice(2 * head * HD, (2 * head + 1) * HD)
        value = slice((2 * head + 1) * HD, (2 * head + 2) * HD)
        key_grad, value_grad = (
            functools.reduce(jnp.add, [ref[part, :].astype(full) for ref in kv_refs])
            for part in (key, value)
        )
        to_key = span + 2 * head * HD
        joined[to_key : to_key + HD, :] = rotated_back(key_grad).astype(low)
        joined[to_key + HD : to_key + 2 * HD, :] = value_grad.astype(low)

    gain_sum, shift_sum = jnp.zeros((1, width), full), jnp.zeros((1, width), full)
    gain = gain_ref[...]
    for piece in range(TP):
        at = slice(piece * block, (piece + 1) * block)
        x = x_refs[piece][...].astype(full)
        centred = x - jnp.mean(x, axis=1, keepdims=True)
        spread = jnp.mean(centred * centred, axis=1, keepdims=True)
        normed = centred * lax.rsqrt(spread + norm_eps)
        first_gradient = dot(joined[:, at].T, matrix_ref[...])
        gain_sum += jnp.sum(first_gradient * normed, axis=0, keepdims=True)
        shift_sum += jnp.sum(first_gradient, axis=0, keepdims=True)
        slope = first_gradient * gain + slope_in_ref[at, :]
        slope_ref[part_ref[0] ^ piece] = slope.astype(low)

    gradient[...] = dot(joined[...], first_ref[...]).astype(low)
    order = order_ref[...]
    joined_rows = dot(order, gradient[...], ((1,), (1,))).astype(low)
    sums = jnp.concatenate(
        [gain_sum, shift_sum, early_ref[2:, :], jnp.zeros((HD - early_ref.shape[0], width), full)],
        axis=0,
    )
    sums = dot(order, sums.astype(low), ((1,), (1,)))
    joined_sum = jnp.sum(joined[...].astype(full), axis=1, keepdims=True)
    joined_sum = jnp.broadcast_to(joined_sum, (3 * span, HD)).astype(low)
    lane = lax.broadcasted_iota(jnp.int32, (width, HD), 1)
    for k in range(3):
        chosen = (source_ref[...] == 3 * place_ref[...] + k).astype(full).astype(low)
        sums = jnp.where(lane == 5 + k, dot(chosen, joined_sum), sums)
    half = width // 2
    for ref, at in ((kept_ref, slice(half)), (sent_ref, slice(half, width))):
        ref[:, : 3 * span] = joined_rows[at]
        ref[:, 3 * span : 3 * span + HD] = sums[at].astype(low)
        ref[:, 3 * span + HD :] = merge_ref[at, :]


def finish(
    heads,
    part,
    order,
    place,
    source,
    cosines,
    sines,
    matrix,
    gain,
    early,
    q_grad,
    first_low,
    slope,
    merge_rows,
    x_pieces,
    kv_grads,
):
    block, width = x_pieces[0].shape
    count, span = TP * block, heads * HD
    return pl.pallas_call(
        functools.partial(finish_kernel, heads),
        out_shape=(
            jax.ShapeDtypeStruct((width // 2, 3 * span + HD + width), low),
            jax.ShapeDtypeStruct((width // 2, 3 * span + HD + width), low),
            jax.ShapeDtypeStruct((TP, block, width), low),
        ),
        in_specs=[pl.BlockSpec(memory_space=pltpu.SMEM)]
        + [pl.BlockSpec(memory_space=pltpu.VMEM)] * (12 + TP + len(kv_grads)),
        scratch_shapes=[pltpu.VMEM((3 * span, width), low), pltpu.VMEM((3 * span, count), low)],
        compiler_params=pltpu.CompilerParams(vmem_limit_bytes=VMEM),
        cost_estimate=pl.CostEstimate(
            flops=50 * width * span * count, bytes_accessed=16 * count * width, transcendentals=count
        ),
        name="finish",
    )(
        part,
        order,
        place,
        source,
        cosines,
        sines,
        matrix,
        gain,
        early,
        q_grad,
        first_low,
        slope,
        merge_rows,
        *x_pieces,
        *kv_grads,
    )


def tokens_kernel(x_ref, cotangent_ref, slopes_ref, out_ref):
    x = x_ref[...].astype(full)
    centred = x - jnp.mean(x, axis=1, keepdims=True)
    inverse = lax.rsqrt(jnp.mean(centred * centred, axis=1, keepdims=True) + norm_eps)
    normed = centred * inverse
    slope = functools.reduce(jnp.add, [slopes_ref[part].astype(full) for part in range(TP)])
    slope_mean = jnp.mean(slope, axis=1, keepdims=True)
    along = jnp.mean(slope * normed, axis=1, keepdims=True)
    out_ref[...] = cotangent_ref[...].astype(full) + inverse * (slope - slope_mean - normed * along)


def tokens_gradient(x_low, cotangent, slopes):
    return pl.pallas_call(
        tokens_kernel,
        out_shape=jax.ShapeDtypeStruct(x_low.shape, full),
        compiler_params=pltpu.CompilerParams(vmem_limit_bytes=VMEM),
        name="tokens_gradient",
    )(x_low, cotangent, slopes)


def on_device(
    tokens,
    positions,
    gain_attention,
    bias_attention,
    gain_feed,
    bias_feed,
    weight_joined,
    bias_joined,
    weight_merge,
    bias_merge,
    weight_expand,
    bias_expand,
    weight_reduce,
    bias_reduce,
    cotangent,
):
    seqs, block, width = tokens.shape
    units = weight_expand.shape[1]
    copies = lax.axis_size("dp")
    members = lax.axis_size("blk")
    groups = members // TP
    here = lax.axis_index("blk")
    my_part, my_group, my_copy = here // groups, here % groups, lax.axis_index("dp")
    heads = width // HD // TP
    depth = weight_joined.shape[0]
    part_units = units // TP
    my_units = weight_reduce.shape[0]
    span = heads * HD

    def over_parts(value, away):
        return lax.ppermute(value, "blk", [(i, i ^ (away * groups)) for i in range(members)])

    def over_groups(value, away):
        return lax.ppermute(value, "blk", [(i, i ^ away) for i in range(members)])

    def over_copies(value, away):
        return lax.ppermute(value, "dp", [(i, i ^ away) for i in range(copies)])

    part_lines = [[part * groups + g for part in range(TP)] for g in range(groups)]
    group_planes = [[part * groups + g for g in range(groups)] for part in range(TP)]

    def swapped(value, lines):
        return lax.all_to_all(value, "blk", 0, 0, axis_index_groups=lines, tiled=True)

    def from_mine(value, me, axis):
        count = value.shape[axis]
        bit = 1
        while bit < count:
            split = value.reshape(value.shape[:axis] + (-1, 2, bit) + value.shape[axis + 1 :])
            flipped = jnp.flip(split, axis + 1).reshape(value.shape)
            value = jnp.where(me // bit % 2 == 1, flipped, value)
            bit *= 2
        return value

    def picked(value, at, axis):
        return lax.dynamic_index_in_dim(value, at, axis, keepdims=False)

    def exchanged(value, move, count, me, axis):
        return [picked(value, me, axis)] + [
            move(picked(value, me ^ away, axis), away) for away in range(1, count)
        ]

    def halved(value, move, count, me):
        while count > 1:
            count //= 2
            halves = value.reshape((2, count) + value.shape[1:])
            upper = me // count % 2
            sent = move(picked(halves, 1 - upper, 0).astype(low), count)
            value = picked(halves, upper, 0).astype(full) + sent.astype(full)
        return value[0]

    def ready(value):
        first = value[(0,) * value.ndim]
        return first == first

    def added(pieces):
        return functools.reduce(jnp.add, [piece.astype(full) for piece in pieces])

    def placed(pieces, me):
        out = jnp.zeros((len(pieces),) + pieces[0].shape, pieces[0].dtype)
        for away, piece in enumerate(pieces):
            out = lax.dynamic_update_index_in_dim(out, piece, me ^ away, 0)
        return out

    def of_group(value):
        return jnp.concatenate([value] + [over_parts(value, away) for away in range(1, TP)], axis=0)

    count = TP * block
    runs = count // RUN

    def as_columns(vector):
        return vector.reshape(depth, -1)

    starts = (positions.reshape(-1)[::RUN] // RUN).astype(low)
    starts = jnp.pad(starts, (0, depth - starts.shape[0]))
    small = jnp.concatenate(
        [
            as_columns(vector)
            for vector in (
                gain_attention,
                bias_attention,
                gain_feed,
                bias_feed,
                bias_merge,
                bias_reduce,
                bias_joined,
                bias_expand,
                starts,
            )
        ],
        axis=1,
    )
    small = jnp.pad(small, ((0, 0), (0, HD - small.shape[1])))

    def by_head(matrix):
        lead = matrix.shape[:-1]
        split = matrix.reshape(lead + (3, TP, heads, HD))
        queries = split[..., 0, :, :, :].reshape(lead + (TP, span))
        kv = jnp.stack([split[..., 1, :, :, :], split[..., 2, :, :, :]], axis=-2)
        return jnp.concatenate([queries, kv.reshape(lead + (TP, 2 * span))], axis=-1)

    def from_head(matrix):
        lead = matrix.shape[:-2]
        queries = matrix[..., :span].reshape(lead + (1, TP, heads, HD))
        kv = matrix[..., span:].reshape(lead + (TP, heads, 2, HD))
        kv = jnp.moveaxis(kv, -2, len(lead))
        return jnp.concatenate([queries, kv], axis=len(lead)).reshape(lead + (3 * width,))

    expand_parts = weight_expand.reshape(depth, copies, TP, groups * my_units)
    expand_parts = jnp.moveaxis(expand_parts, 2, 0).reshape(TP, depth, part_units)
    parts = jnp.concatenate(
        [
            expand_parts,
            jnp.broadcast_to(weight_merge, (TP, depth, width)),
            jnp.swapaxes(by_head(weight_joined), 0, 1),
            jnp.broadcast_to(small, (TP, depth, HD)),
        ],
        axis=2,
    )
    tokens = jnp.where(ready(parts), tokens, jnp.zeros_like(tokens))
    to_merge, to_joined = part_units, part_units + width
    to_small = 3 * span
    mine = swapped(parts, part_lines).reshape(my_units, -1)
    own_low = tokens.reshape(block, width)
    own_later, _ = lax.optimization_barrier((own_low, mine))
    x_pieces = [own_low, over_parts(own_low, 1)]
    x_pieces += [over_parts(own_later, away) for away in range(2, TP)]
    rows = own_low.astype(full)
    first_rows = mine[:, to_joined:]
    mine = jnp.concatenate([mine[:, :to_joined], weight_reduce], axis=1)
    def in_plane(value):
        value = swapped(jnp.broadcast_to(value, (groups,) + value.shape), group_planes)
        return value.reshape(groups * my_units, -1)

    def of_copies(value):
        return [value] + [over_copies(value, away) for away in range(1, copies)]

    near = in_plane(first_rows)
    row_pieces = of_copies(near)
    rest_pieces = of_copies(in_plane(mine))
    up_low, *_ = lax.optimization_barrier((cotangent, *x_pieces[1:]))
    up_low = up_low.reshape(block, width)
    up_pieces = [up_low] + [over_parts(up_low, away) for away in range(1, TP)]
    came = jnp.arange(width, dtype=jnp.int32)
    row, came_part = came % depth, (came // depth) % TP
    came_group = (came // (depth * TP)) % groups
    came_copy = came // (depth * TP * groups) ^ my_copy
    place_of = ((came_copy * TP + came_part) * groups + came_group) * depth + row
    wanted = jnp.arange(width, dtype=jnp.int32)[:, None]
    order = (place_of[None, :] == wanted).astype(low)
    back_order = (place_of[:, None] == wanted[:, 0]).astype(low)
    source = jnp.arange(3 * width, dtype=jnp.int32)
    unit = jnp.arange(part_units, dtype=jnp.int32)
    unit_group = (unit // my_units) % groups
    unit_copy = unit // (my_units * groups) ^ my_copy
    unit_place = (unit_copy * groups + unit_group) * my_units + unit % my_units
    unit_order = (unit_place[None, :] == unit[:, None]).astype(low)

    unit_back_order = (unit_place[:, None] == unit[None, :]).astype(low)
    head_order = lax.dynamic_slice_in_dim(order, my_part * span, span, 0)

    run_starts = near[:, to_small + 13].reshape(groups, TP, depth)
    run_starts = from_mine(from_mine(run_starts, my_group, 0), my_part, 1)
    k_runs = run_starts[:, :, : block // RUN].astype(jnp.int32).reshape(groups, runs)
    q_runs = k_runs[0]
    places = (q_runs[:, None] * RUN + jnp.arange(RUN, dtype=jnp.int32)).reshape(count)

    half_dims = ROT // 2
    frequency = jnp.exp(jnp.arange(half_dims, dtype=full) * (-2.0 * math.log(10000.0) / ROT))
    angles = frequency[:, None] * places.astype(full)
    cosines, sines = jnp.cos(angles), jnp.sin(angles)
    my_source = picked(by_head(source), my_part, 0)
    queries, kv, first_low, second_low, joined_matrix, small_all = prepare(
        heads, order, my_source[:, None], cosines, sines, x_pieces, row_pieces
    )
    gain_one, _, gain_two, _, merge_shift, reduce_shift = small_all[:6]
    expand_shift = jnp.swapaxes(small_all[9:13], 0, 1)
    expand_shift = picked(expand_shift.reshape(copies, TP, groups * my_units), my_part, 1)
    expand_shift = expand_shift.reshape(-1)
    rank = jnp.sum(q_runs[None, :] < q_runs[:, None], axis=1)
    index = jnp.arange(runs, dtype=jnp.int32)
    q_order = jnp.sum(jnp.where(rank[None, :] == index[:, None], index[None, :], 0), axis=1)
    kv_parts = [kv] + [over_groups(kv, away) for away in range(1, groups)]

    tables = (q_runs, q_order.astype(jnp.int32), k_runs.reshape(-1))
    def sent_halves(value, move, count):
        while count > 1:
            count //= 2
            value = value.reshape((2, -1) + value.shape[1:])
            value = value[0].astype(full) + move(value[1].astype(low), count).astype(full)
        return value

    def over_copies_halved(kept, sent):
        value = kept.astype(full) + over_copies(sent, copies // 2).astype(full)
        return sent_halves(value, over_copies, copies // 2).astype(low)

    def over_plane(value):
        return swapped(value.reshape(groups, my_units, -1), group_planes)

    attended_gradient, merge_matrix, fed, second_slope, feed_sums, *later = feed(
        heads,
        my_part[None].astype(jnp.int32),
        (order, back_order, unit_order, unit_back_order),
        gain_two[None, :],
        expand_shift[None, :],
        second_low,
        x_pieces,
        up_pieces,
        rest_pieces,
    )
    kv_parts, later = lax.optimization_barrier((kv_parts, later))
    later = over_plane(over_copies_halved(*later))

    attended_low, kv_sorted, kv_turned, log_totals, deltas, *branches = attend(
        tables, queries, attended_gradient, merge_matrix, fed, kv_parts
    )
    log_totals, later = lax.optimization_barrier((log_totals, later))
    query_total, kv_totals = attend_back(
        tables, queries, attended_gradient, kv_sorted, kv_turned, log_totals, deltas
    )

    def of_rows(pieces):
        return [pieces[0]] + [over_parts(pieces[away], away) for away in range(1, TP)]

    branches, _ = lax.optimization_barrier((of_rows(branches), query_total))
    branches = added(branches)
    result = (rows + branches + merge_shift + reduce_shift).astype(low)

    attended_then, kv_totals, _, _ = lax.optimization_barrier(
        (attended_low, kv_totals, query_total, result)
    )
    later = jnp.sum(later.astype(full), axis=0)
    gradient_weight_reduce = later[:, part_units:]
    merge_rows = dot(attended_then, jnp.concatenate(up_pieces, axis=0)).astype(low)
    merge_rows = dot(head_order, merge_rows, ((0,), (0,))).astype(low)
    later = later[:, :part_units].astype(low)

    upstream = cotangent.reshape(block, width).astype(full)
    expand_sum = feed_sums[2].reshape(copies, -1)
    expand_sum = jnp.swapaxes(placed_alone(expand_sum, my_part, TP), 0, 1).reshape(width, -1)
    nothing = jnp.zeros((width,), full)
    early = [nothing, nothing, feed_sums[0], feed_sums[1], jnp.sum(upstream, axis=0)]
    early = jnp.stack(early + [nothing] * 3)
    early = jnp.concatenate([early, expand_sum.T], axis=0)
    kv_grads = [kv_totals[0]] + [over_groups(kv_totals[r], r) for r in range(1, groups)]
    final_kept, final_sent, slopes = finish(
        heads,
        my_part[None].astype(jnp.int32),
        back_order,
        place_of[:, None],
        my_source[None, :],
        cosines,
        sines,
        joined_matrix,
        gain_one[None, :],
        early,
        query_total,
        first_low,
        second_slope,
        merge_rows,
        x_pieces,
        kv_grads,
    )
    slopes = swapped(slopes, part_lines)
    gradient_tokens = tokens_gradient(own_low, cotangent.reshape(block, width), slopes)

    final = over_copies_halved(final_kept, final_sent).reshape(groups, my_units, -1)
    final = added(exchanged(final, over_groups, groups, my_group, 0)).astype(low)
    final, _ = lax.optimization_barrier((final, slopes))
    final = jnp.concatenate([final, later], axis=1).reshape(TP, depth, -1)
    final = placed(exchanged(final, over_parts, TP, my_part, 0), my_part)
    to_rest = 3 * span + HD
    gradient_weight_joined = from_head(jnp.swapaxes(final[..., : 3 * span], 0, 1))
    small_total = jnp.sum(final[..., 3 * span : to_rest].astype(full), axis=0)
    gradient_weight_merge = jnp.sum(final[..., to_rest : to_rest + width].astype(full), axis=0)
    gradient_weight_expand = final[..., to_rest + width :]
    gradient_weight_expand = jnp.moveaxis(
        gradient_weight_expand.reshape(TP, depth, copies, groups * my_units), 0, 2
    ).reshape(depth, units)
    gradients = small_total[:, :5].T
    gradient_bias_joined = small_total[:, 5:8].reshape(-1)
    gradient_bias_expand = small_total[:, 8:12].reshape(-1)

    def wide(value):
        return value.astype(full)

    return (
        result.reshape(tokens.shape),
        gradient_tokens.reshape(tokens.shape),
        gradients[0],
        gradients[1],
        gradients[2],
        gradients[3],
        wide(gradient_weight_joined),
        gradient_bias_joined,
        wide(gradient_weight_merge),
        gradients[4],
        wide(gradient_weight_expand),
        gradient_bias_expand,
        wide(gradient_weight_reduce),
        gradients[4],
    )


def placed_alone(value, at, count):
    out = jnp.zeros((count,) + value.shape, value.dtype)
    return lax.dynamic_update_index_in_dim(out, value, at, 0)


def solution(mesh):
    rows = P("dp", "blk", None)
    vector, matrix = P(("dp", "blk")), P(("dp", "blk"), None)
    params = (vector,) * 4 + (matrix, vector) * 4
    return jax.shard_map(
        on_device,
        mesh=mesh,
        in_specs=(rows, P("dp", "blk")) + params + (rows,),
        out_specs=(rows, rows) + params,
        check_vma=False,
    )
```

```python
import functools
import math

import jax
import jax.numpy as jnp
from jax import lax
from jax.experimental import pallas as pl
from jax.experimental.pallas import tpu as pltpu
from jax.sharding import PartitionSpec as P

HD = 64
ROT = 16
TP = 4
RUN = 128
TILE = 2 * RUN
FORWARD_KEYS, FORWARD_REST = 1024, 1024
BACKWARD_KEYS, BACKWARD_REST = 1024, 512
VMEM = 56 * 2**20

norm_eps = 1e-05
masked_score = -1e30
low = jnp.bfloat16
full = jnp.float32


def dot(a, b, dims=((1,), (0,))):
    return lax.dot_general(a, b, (dims, ((), ())), preferred_element_type=full)


def tile_of(tile, q_runs_ref, q_order_ref):
    early, late = q_order_ref[2 * tile], q_order_ref[2 * tile + 1]
    early_run, late_run = q_runs_ref[early], q_runs_ref[late]
    rows = [pl.ds(pl.multiple_of(run * RUN, RUN), RUN) for run in (early, late)]
    column = lax.broadcasted_iota(jnp.int32, (1, TILE), 1)
    places = jnp.where(column < RUN, early_run * RUN + column, late_run * RUN + column - RUN)
    return rows, places, early_run * RUN, late_run * RUN + RUN


def over_keys(step, by_all, by_some, many, few, carry):
    blocks = lax.div(by_all, many)
    carry = lax.fori_loop(0, blocks, functools.partial(step, False, many), carry)
    first = blocks * (many // few)
    last = lax.div(by_some + few - 1, few)
    return lax.fori_loop(first, last, functools.partial(step, True, few), carry)


def columns_of(ref, rows, part=slice(None)):
    return jnp.concatenate([ref[part, at] for at in rows], axis=1)


def hidden(scores, first, places):
    k_places = first + lax.broadcasted_iota(jnp.int32, scores.shape, 0)
    return jnp.where(k_places <= places, scores, masked_score)


def forward_kernel(
    heads, groups, runs, q_runs_ref, q_order_ref, k_runs_ref, q_ref, o_grad_ref, *refs
):
    merge_ref, fed_ref, *kv_refs = refs[: groups + 2]
    out_ref, kv, kv_turned, log_ref, delta_ref, *branch_refs = refs[groups + 2 : -3]
    first_w, state, out_total = refs[-3:]
    pair = 2 * HD

    for source in range(groups):

        def place(run, carry, source=source):
            at = pl.multiple_of(k_runs_ref[source * runs + run] * RUN, RUN)
            columns = kv_refs[source][:, pl.ds(pl.multiple_of(run * RUN, RUN), RUN)]
            kv_turned[:, pl.ds(at, RUN)] = columns
            for head in range(heads):
                part = slice(head * pair, (head + 1) * pair)
                kv[pl.ds(at, RUN), part] = columns[part, :].T
            return carry

        lax.fori_loop(0, runs, place, 0)

    def tile_step(tile, carry):
        rows, places, by_all, by_some = tile_of(tile, q_runs_ref, q_order_ref)
        nothing = jnp.zeros((HD, TILE), low)
        for head in range(heads):
            part = slice(head * HD, (head + 1) * HD)
            first_w[head] = jnp.concatenate([columns_of(q_ref, rows, part), nothing], axis=0)
        state[...] = jnp.full(state.shape, masked_score, full)
        out_total[...] = jnp.zeros_like(out_total)

        def step(hides, size, block, sums):
            at = pl.ds(pl.multiple_of(block * size, size), size)
            new_sums = []
            products = [
                dot(kv[at, head * pair : (head + 1) * pair], first_w[head]) for head in range(heads)
            ]
            for head in range(heads):
                scores = products[head]
                if hides:
                    scores = hidden(scores, block * size, places)
                old_max = state[head : head + 1, :]
                new_max = jnp.maximum(old_max, jnp.max(scores, axis=0, keepdims=True))
                weights = jnp.exp(scores - new_max)
                fading = jnp.exp(old_max - new_max)
                state[head : head + 1, :] = new_max
                new_sums.append(sums[head] * fading + jnp.sum(weights, axis=0, keepdims=True))
                here = slice(head * HD, (head + 1) * HD)
                values = kv_turned[head * pair + HD : (head + 1) * pair, at]
                out_total[here, :] = out_total[here, :] * fading + dot(values, weights.astype(low))
            return tuple(new_sums)

        sums = tuple(jnp.zeros((1, TILE), full) for _ in range(heads))
        sums = over_keys(step, by_all, by_some, FORWARD_KEYS, FORWARD_REST, sums)
        for head in range(heads):
            here = slice(head * HD, (head + 1) * HD)
            attended = out_total[here, :] / sums[head]
            log_total = state[head : head + 1, :] + jnp.log(sums[head])
            o_grad = columns_of(o_grad_ref, rows, here).astype(full)
            delta = jnp.sum(o_grad * attended, axis=0, keepdims=True)
            for half, at in enumerate(rows):
                columns = slice(half * RUN, (half + 1) * RUN)
                out_ref[here, at] = attended[:, columns].astype(low)
                log_ref[head : head + 1, at] = log_total[:, columns]
                delta_ref[head : head + 1, at] = delta[:, columns]
        return carry

    lax.fori_loop(0, q_ref.shape[1] // TILE, tile_step, 0)

    block = branch_refs[0].shape[0]
    for piece, ref in enumerate(branch_refs):
        at = slice(piece * block, (piece + 1) * block)
        branch = dot(out_ref[:, at].T, merge_ref[...]) + fed_ref[at, :]
        ref[...] = branch.astype(ref.dtype)


def halves_of(groups, half):
    steps = [2**k for k in range(groups.bit_length() - 1)]
    steps = steps[::-1] if half else steps
    kept = [0]
    for away in steps[:-1]:
        kept = kept + [source ^ away for source in kept]
    return kept, [source ^ steps[-1] for source in kept], steps[::-1]


def backward_kernel(
    heads,
    groups,
    runs,
    q_runs_ref,
    q_order_ref,
    k_runs_ref,
    q_ref,
    o_grad_ref,
    kv,
    kv_turned,
    log_ref,
    delta_ref,
    q_grad_ref,
    *refs,
):
    kv_grad_refs = refs[:4]
    total, first_w, second_w, q_total = refs[4:]
    pair = 2 * HD
    total[...] = jnp.zeros_like(total)

    def tile_step(tile, carry):
        rows, places, by_all, by_some = tile_of(tile, q_runs_ref, q_order_ref)
        nothing = jnp.zeros((HD, TILE), low)
        for head in range(heads):
            part = slice(head * HD, (head + 1) * HD)
            upper = jnp.concatenate([columns_of(q_ref, rows, part), nothing], axis=0)
            lower = jnp.concatenate([nothing, columns_of(o_grad_ref, rows, part)], axis=0)
            first_w[head, :, :TILE] = upper
            first_w[head, :, TILE:] = lower
            second_w[head, :TILE, :] = upper.T
            second_w[head, TILE:, :] = lower.T
        q_total[...] = jnp.zeros_like(q_total)
        log_totals = columns_of(log_ref, rows)
        deltas = columns_of(delta_ref, rows)

        def step(hides, size, block, carry):
            at = pl.ds(pl.multiple_of(block * size, size), size)
            products = [
                dot(kv[at, head * pair : (head + 1) * pair], first_w[head]) for head in range(heads)
            ]
            for head in range(heads):
                part = slice(head * pair, (head + 1) * pair)
                both = products[head]
                scores = both[:, :TILE]
                if hides:
                    scores = hidden(scores, block * size, places)
                chances = jnp.exp(scores - log_totals[head : head + 1, :])
                score_grad = chances * (both[:, TILE:] - deltas[head : head + 1, :])
                score_grad = score_grad.astype(low)
                joint = jnp.concatenate([score_grad, chances.astype(low)], axis=1)
                total[at, part] += dot(joint, second_w[head])
                here = slice(head * HD, (head + 1) * HD)
                keys = kv_turned[head * pair : head * pair + HD, at]
                q_total[here, :] += dot(keys, score_grad)
            return carry

        over_keys(step, by_all, by_some, BACKWARD_KEYS, BACKWARD_REST, 0)
        for half, at in enumerate(rows):
            q_grad_ref[:, at] = q_total[:, half * RUN : (half + 1) * RUN]
        return carry

    lax.fori_loop(0, q_ref.shape[1] // TILE, tile_step, 0)

    half_runs = runs // 2
    for half in range(2):
        kept, sent, _ = halves_of(groups, half)
        for ref, sources in zip(kv_grad_refs[2 * half : 2 * half + 2], (kept, sent)):
            for slot, source in enumerate(sources):

                def give(run, carry, ref=ref, slot=slot, first=source * runs + half * half_runs):
                    at = pl.multiple_of(k_runs_ref[first + run] * RUN, RUN)
                    columns = pl.ds(pl.multiple_of(run * RUN, RUN), RUN)
                    rows = total[pl.ds(at, RUN), :].astype(low)
                    for head in range(heads):
                        part = slice(head * pair, (head + 1) * pair)
                        ref[slot, part, columns] = rows[:, part].T
                    return carry

                lax.fori_loop(0, half_runs, give, 0)


def attention_call(kernel, name, tables, operands, out_shape, scratch, groups, work):
    width, count = operands[0].shape
    heads, runs = width // HD, count // RUN
    pairs = count * groups * count * heads // 2
    smem = pl.BlockSpec(memory_space=pltpu.SMEM)
    vmem = pl.BlockSpec(memory_space=pltpu.VMEM)
    return pl.pallas_call(
        functools.partial(kernel, heads, groups, runs),
        out_shape=out_shape,
        in_specs=[smem] * len(tables) + [vmem] * len(operands),
        out_specs=tuple([vmem] * len(out_shape)),
        scratch_shapes=scratch,
        compiler_params=pltpu.CompilerParams(vmem_limit_bytes=VMEM),
        cost_estimate=pl.CostEstimate(
            flops=work * pairs,
            bytes_accessed=8 * count * width * groups,
            transcendentals=pairs,
        ),
        name=name,
    )(*tables, *operands)


def pieces_of(block, width):
    kept = jax.ShapeDtypeStruct((block, width), full)
    return (kept,) + (jax.ShapeDtypeStruct((block, width), low),) * (TP - 1)


def attend(tables, queries, o_grads, merge_matrix, fed, kv_parts):
    width, count = queries.shape
    keys = len(kv_parts) * count
    out_shape = (
        jax.ShapeDtypeStruct((width, count), low),
        jax.ShapeDtypeStruct((keys, 2 * width), low),
        jax.ShapeDtypeStruct((2 * width, keys), low),
        jax.ShapeDtypeStruct((8, count), full),
        jax.ShapeDtypeStruct((8, count), full),
    ) + pieces_of(count // TP, fed.shape[1])
    scratch = [
        pltpu.VMEM((width // HD, 2 * HD, TILE), low),
        pltpu.VMEM((8, TILE), full),
        pltpu.VMEM((width, TILE), full),
    ]
    operands = (queries, o_grads, merge_matrix, fed) + tuple(kv_parts)
    groups = len(kv_parts)
    return attention_call(
        forward_kernel, "attend", tables, operands, out_shape, scratch, groups, 6000
    )


def attend_back(tables, queries, o_grads, kv, kv_turned, log_totals, deltas):
    width, count = queries.shape
    keys = kv.shape[0]
    groups = keys // count
    out_shape = (jax.ShapeDtypeStruct((width, count), full),) + (
        jax.ShapeDtypeStruct((groups // 2, 2 * width, count // 2), low),
    ) * 4
    scratch = [
        pltpu.VMEM((keys, 2 * width), full),
        pltpu.VMEM((width // HD, 2 * HD, 2 * TILE), low),
        pltpu.VMEM((width // HD, 2 * TILE, 2 * HD), low),
        pltpu.VMEM((width, TILE), full),
    ]
    operands = (queries, o_grads, kv, kv_turned, log_totals, deltas)
    out = attention_call(
        backward_kernel, "attend_back", tables, operands, out_shape, scratch, groups, 6000
    )
    return out[0], out[1:]


def prepare_kernel(heads, order_ref, source_ref, cosine_ref, sine_ref, *refs):
    x_refs, piece_refs, outs = refs[:TP], refs[TP:-6], refs[-6:]
    q_ref, kv_ref, first_ref, second_ref, matrix_ref, small_ref = outs
    span = heads * HD
    block, width = x_refs[0].shape
    rows = jnp.concatenate([piece[...] for piece in piece_refs], axis=0)
    columns = dot(order_ref[...], rows).astype(low)
    turned_columns = columns.T
    matrix = turned_columns[: 3 * span]
    small = turned_columns[3 * span :].astype(full)
    matrix_ref[...] = matrix
    small_ref[...] = small
    gain_one, shift_one, gain_two, shift_two = (small[k : k + 1] for k in range(4))

    shift = jnp.zeros((3 * span, 1), full)
    lane = lax.broadcasted_iota(jnp.int32, (3 * span, HD), 1)
    feature = lax.broadcasted_iota(jnp.int32, (3 * span, width), 1)
    for k in range(3):
        chosen = (source_ref[...] == 3 * feature + k).astype(full).astype(low)
        found = dot(chosen, columns[:, 3 * span :])
        shift += jnp.sum(jnp.where(lane == 6 + k, found, 0.0), axis=1, keepdims=True)

    cosines, sines = cosine_ref[...], sine_ref[...]
    half_dims = ROT // 2

    def rotated(head, at):
        cosine, sine = cosines[:, at], sines[:, at]
        first, second = head[:half_dims], head[half_dims:ROT]
        return jnp.concatenate(
            [first * cosine - second * sine, second * cosine + first * sine, head[ROT:]], axis=0
        )

    for piece in range(TP):
        at = slice(piece * block, (piece + 1) * block)
        x = x_refs[piece][...].astype(full)
        centred = x - jnp.mean(x, axis=1, keepdims=True)
        spread = jnp.mean(centred * centred, axis=1, keepdims=True)
        normed = centred * lax.rsqrt(spread + norm_eps)
        first_low = (normed * gain_one + shift_one).astype(low)
        first_ref[at, :] = first_low
        second_ref[at, :] = (normed * gain_two + shift_two).astype(low)
        joined = dot(matrix, first_low, ((1,), (1,))) + shift
        for head in range(heads):
            here = slice(head * HD, (head + 1) * HD)
            queries = rotated(joined[here], at).astype(low)
            q_ref[here, at] = queries * jnp.asarray(HD**-0.5, low)
            to_key = span + 2 * head * HD
            to_value = to_key + HD
            kv_ref[2 * head * HD : (2 * head + 1) * HD, at] = rotated(
                joined[to_key:to_value], at
            ).astype(low)
            kv_ref[(2 * head + 1) * HD : (2 * head + 2) * HD, at] = joined[
                to_value : to_value + HD
            ].astype(low)


def prepare(heads, order, source, cosines, sines, x_pieces, row_pieces):
    block, width = x_pieces[0].shape
    count, span = TP * block, heads * HD
    return pl.pallas_call(
        functools.partial(prepare_kernel, heads),
        out_shape=(
            jax.ShapeDtypeStruct((span, count), low),
            jax.ShapeDtypeStruct((2 * span, count), low),
            jax.ShapeDtypeStruct((count, width), low),
            jax.ShapeDtypeStruct((count, width), low),
            jax.ShapeDtypeStruct((3 * span, width), low),
            jax.ShapeDtypeStruct((HD, width), full),
        ),
        compiler_params=pltpu.CompilerParams(vmem_limit_bytes=VMEM),
        cost_estimate=pl.CostEstimate(
            flops=50 * width * span * count, bytes_accessed=16 * count * width, transcendentals=count
        ),
        name="prepare",
    )(order, source, cosines, sines, *x_pieces, *row_pieces)


def feed_kernel(
    heads,
    part_ref,
    order_ref,
    back_order_ref,
    unit_order_ref,
    unit_back_order_ref,
    gain_ref,
    shift_ref,
    second_ref,
    *refs,
):
    x_refs, up_refs, piece_refs, refs = refs[:TP], refs[TP : 2 * TP], refs[2 * TP : -11], refs[-11:]
    o_grad_ref, merge_ref, fed_ref, slope_ref, sums_ref, kept_ref, sent_ref = refs[:7]
    expand, reduce, active, gradient = refs[7:]
    span = heads * HD
    block, width = x_refs[0].shape
    units = expand.shape[1]
    rows = jnp.concatenate([piece[...] for piece in piece_refs], axis=0)
    expand[...] = dot(order_ref[...], rows[:, :units]).astype(low)
    reduce[...] = dot(unit_order_ref[...], rows[:, units + width :]).astype(low)
    mine = pl.ds(pl.multiple_of(part_ref[0] * span, span), span)
    merge_ref[...] = dot(order_ref[mine, :], rows[:, units : units + width]).astype(low)
    sums = [jnp.zeros((1, width), full)] * 2 + [jnp.zeros((1, units), full)]
    for piece in range(TP):
        at = slice(piece * block, (piece + 1) * block)
        up = up_refs[piece][...]
        expanded = dot(second_ref[at, :], expand[...]) + shift_ref[...]
        normal = 0.5 + 0.5 * lax.erf(expanded * 0.5**0.5)
        active_low = (expanded * normal).astype(low)
        active[at, :] = active_low
        fed_ref[at, :] = dot(active_low, reduce[...])
        o_grad_ref[:, at] = dot(merge_ref[...], up, ((1,), (1,))).astype(low)
        density = jnp.exp(-0.5 * expanded * expanded) * (2 * math.pi) ** -0.5
        expanded_gradient = dot(up, reduce[...], ((1,), (1,))) * (normal + expanded * density)
        gradient_low = expanded_gradient.astype(low)
        gradient[at, :] = gradient_low
        sums[2] += jnp.sum(gradient_low.astype(full), axis=0, keepdims=True)
        second_gradient = dot(gradient_low, expand[...], ((1,), (1,)))
        x = x_refs[piece][...].astype(full)
        centred = x - jnp.mean(x, axis=1, keepdims=True)
        spread = jnp.mean(centred * centred, axis=1, keepdims=True)
        normed = centred * lax.rsqrt(spread + norm_eps)
        sums[0] += jnp.sum(second_gradient * normed, axis=0, keepdims=True)
        sums[1] += jnp.sum(second_gradient, axis=0, keepdims=True)
        slope_ref[at, :] = second_gradient * gain_ref[...]
    sums_ref[...] = jnp.concatenate(sums + [jnp.zeros((5, width), full)], axis=0)
    up = jnp.concatenate([ref[...] for ref in up_refs], axis=0)
    expand_rows = dot(second_ref[...].T, gradient[...]).astype(low)
    reduce_rows = dot(active[...].T, up).astype(low)
    expand_rows = dot(back_order_ref[...], expand_rows).astype(low)
    reduce_rows = dot(unit_back_order_ref[...], reduce_rows).astype(low)
    half = width // 2
    for ref, at in ((kept_ref, slice(half)), (sent_ref, slice(half, width))):
        ref[:, :units] = expand_rows[at]
        ref[:, units:] = reduce_rows[at]


def feed(heads, part, orders, gain, shift, second_low, x_pieces, up_pieces, row_pieces):
    block, width = x_pieces[0].shape
    count, span, units = TP * block, heads * HD, shift.shape[1]
    rows_shape = jax.ShapeDtypeStruct((width // 2, units + width), low)
    operands = (*orders, gain, shift, second_low, *x_pieces, *up_pieces, *row_pieces)
    vmem = pl.BlockSpec(memory_space=pltpu.VMEM)
    return pl.pallas_call(
        functools.partial(feed_kernel, heads),
        out_shape=(
            jax.ShapeDtypeStruct((span, count), low),
            jax.ShapeDtypeStruct((span, width), low),
            jax.ShapeDtypeStruct((count, width), full),
            jax.ShapeDtypeStruct((count, width), full),
            jax.ShapeDtypeStruct((8, width), full),
            rows_shape,
            rows_shape,
        ),
        in_specs=[pl.BlockSpec(memory_space=pltpu.SMEM)] + [vmem] * len(operands),
        out_specs=(vmem,) * 7,
        scratch_shapes=[
            pltpu.VMEM((width, units), low),
            pltpu.VMEM((units, width), low),
            pltpu.VMEM((count, units), low),
            pltpu.VMEM((count, units), low),
        ],
        compiler_params=pltpu.CompilerParams(vmem_limit_bytes=VMEM),
        cost_estimate=pl.CostEstimate(flops=0, bytes_accessed=0, transcendentals=0),
        name="feed",
    )(part, *operands)


def finish_kernel(
    heads,
    part_ref,
    order_ref,
    place_ref,
    source_ref,
    cosine_ref,
    sine_ref,
    matrix_ref,
    gain_ref,
    early_ref,
    q_grad_ref,
    first_ref,
    slope_in_ref,
    merge_ref,
    *refs,
):
    x_refs, kv_refs, outs = refs[:TP], refs[TP:-5], refs[-5:]
    kept_ref, sent_ref, slope_ref, gradient, joined = outs
    kv_pairs = (kv_refs[:2], kv_refs[2:])
    span = heads * HD
    block, width = x_refs[0].shape
    half_dims = ROT // 2
    cosine, sine = cosine_ref[...], sine_ref[...]

    def rotated_back(head):
        first, second = head[:half_dims], head[half_dims:ROT]
        return jnp.concatenate(
            [first * cosine + second * sine, second * cosine - first * sine, head[ROT:]], axis=0
        )

    for head in range(heads):
        here = slice(head * HD, (head + 1) * HD)
        joined[here, :] = rotated_back(q_grad_ref[here, :] * HD**-0.5).astype(low)
        key = slice(2 * head * HD, (2 * head + 1) * HD)
        value = slice((2 * head + 1) * HD, (2 * head + 2) * HD)
        key_grad, value_grad = (
            jnp.concatenate(
                [kept[part, :] + sent[part, :].astype(full) for kept, sent in kv_pairs], axis=1
            )
            for part in (key, value)
        )
        to_key = span + 2 * head * HD
        joined[to_key : to_key + HD, :] = rotated_back(key_grad).astype(low)
        joined[to_key + HD : to_key + 2 * HD, :] = value_grad.astype(low)

    gain_sum, shift_sum = jnp.zeros((1, width), full), jnp.zeros((1, width), full)
    gain = gain_ref[...]
    for piece in range(TP):
        at = slice(piece * block, (piece + 1) * block)
        x = x_refs[piece][...].astype(full)
        centred = x - jnp.mean(x, axis=1, keepdims=True)
        spread = jnp.mean(centred * centred, axis=1, keepdims=True)
        normed = centred * lax.rsqrt(spread + norm_eps)
        first_gradient = dot(joined[:, at].T, matrix_ref[...])
        gain_sum += jnp.sum(first_gradient * normed, axis=0, keepdims=True)
        shift_sum += jnp.sum(first_gradient, axis=0, keepdims=True)
        slope = first_gradient * gain + slope_in_ref[at, :]
        slope_ref[part_ref[0] ^ piece] = slope.astype(low)

    gradient[...] = dot(joined[...], first_ref[...]).astype(low)
    order = order_ref[...]
    joined_rows = dot(order, gradient[...], ((1,), (1,))).astype(low)
    sums = jnp.concatenate(
        [gain_sum, shift_sum, early_ref[2:, :], jnp.zeros((HD - early_ref.shape[0], width), full)],
        axis=0,
    )
    sums = dot(order, sums.astype(low), ((1,), (1,)))
    joined_sum = jnp.sum(joined[...].astype(full), axis=1, keepdims=True)
    joined_sum = jnp.broadcast_to(joined_sum, (3 * span, HD)).astype(low)
    lane = lax.broadcasted_iota(jnp.int32, (width, HD), 1)
    for k in range(3):
        chosen = (source_ref[...] == 3 * place_ref[...] + k).astype(full).astype(low)
        sums = jnp.where(lane == 5 + k, dot(chosen, joined_sum), sums)
    half = width // 2
    for ref, at in ((kept_ref, slice(half)), (sent_ref, slice(half, width))):
        ref[:, : 3 * span] = joined_rows[at]
        ref[:, 3 * span : 3 * span + HD] = sums[at].astype(low)
        ref[:, 3 * span + HD :] = merge_ref[at, :]


def finish(
    heads,
    part,
    order,
    place,
    source,
    cosines,
    sines,
    matrix,
    gain,
    early,
    q_grad,
    first_low,
    slope,
    merge_rows,
    x_pieces,
    kv_grads,
):
    block, width = x_pieces[0].shape
    count, span = TP * block, heads * HD
    return pl.pallas_call(
        functools.partial(finish_kernel, heads),
        out_shape=(
            jax.ShapeDtypeStruct((width // 2, 3 * span + HD + width), low),
            jax.ShapeDtypeStruct((width // 2, 3 * span + HD + width), low),
            jax.ShapeDtypeStruct((TP, block, width), low),
        ),
        in_specs=[pl.BlockSpec(memory_space=pltpu.SMEM)]
        + [pl.BlockSpec(memory_space=pltpu.VMEM)] * (12 + TP + len(kv_grads)),
        scratch_shapes=[pltpu.VMEM((3 * span, width), low), pltpu.VMEM((3 * span, count), low)],
        compiler_params=pltpu.CompilerParams(vmem_limit_bytes=VMEM),
        cost_estimate=pl.CostEstimate(
            flops=50 * width * span * count, bytes_accessed=16 * count * width, transcendentals=count
        ),
        name="finish",
    )(
        part,
        order,
        place,
        source,
        cosines,
        sines,
        matrix,
        gain,
        early,
        q_grad,
        first_low,
        slope,
        merge_rows,
        *x_pieces,
        *kv_grads,
    )


def tokens_kernel(x_ref, cotangent_ref, slopes_ref, out_ref):
    x = x_ref[...].astype(full)
    centred = x - jnp.mean(x, axis=1, keepdims=True)
    inverse = lax.rsqrt(jnp.mean(centred * centred, axis=1, keepdims=True) + norm_eps)
    normed = centred * inverse
    slope = functools.reduce(jnp.add, [slopes_ref[part].astype(full) for part in range(TP)])
    slope_mean = jnp.mean(slope, axis=1, keepdims=True)
    along = jnp.mean(slope * normed, axis=1, keepdims=True)
    out_ref[...] = cotangent_ref[...].astype(full) + inverse * (slope - slope_mean - normed * along)


def tokens_gradient(x_low, cotangent, slopes):
    return pl.pallas_call(
        tokens_kernel,
        out_shape=jax.ShapeDtypeStruct(x_low.shape, full),
        compiler_params=pltpu.CompilerParams(vmem_limit_bytes=VMEM),
        name="tokens_gradient",
    )(x_low, cotangent, slopes)


def on_device(
    tokens,
    positions,
    gain_attention,
    bias_attention,
    gain_feed,
    bias_feed,
    weight_joined,
    bias_joined,
    weight_merge,
    bias_merge,
    weight_expand,
    bias_expand,
    weight_reduce,
    bias_reduce,
    cotangent,
):
    seqs, block, width = tokens.shape
    units = weight_expand.shape[1]
    copies = lax.axis_size("dp")
    members = lax.axis_size("blk")
    groups = members // TP
    here = lax.axis_index("blk")
    my_part, my_group, my_copy = here // groups, here % groups, lax.axis_index("dp")
    heads = width // HD // TP
    depth = weight_joined.shape[0]
    part_units = units // TP
    my_units = weight_reduce.shape[0]
    span = heads * HD

    def over_parts(value, away):
        return lax.ppermute(value, "blk", [(i, i ^ (away * groups)) for i in range(members)])

    def over_groups(value, away):
        return lax.ppermute(value, "blk", [(i, i ^ away) for i in range(members)])

    def over_copies(value, away):
        return lax.ppermute(value, "dp", [(i, i ^ away) for i in range(copies)])

    part_lines = [[part * groups + g for part in range(TP)] for g in range(groups)]
    group_planes = [[part * groups + g for g in range(groups)] for part in range(TP)]

    def swapped(value, lines):
        return lax.all_to_all(value, "blk", 0, 0, axis_index_groups=lines, tiled=True)

    def from_mine(value, me, axis):
        count = value.shape[axis]
        bit = 1
        while bit < count:
            split = value.reshape(value.shape[:axis] + (-1, 2, bit) + value.shape[axis + 1 :])
            flipped = jnp.flip(split, axis + 1).reshape(value.shape)
            value = jnp.where(me // bit % 2 == 1, flipped, value)
            bit *= 2
        return value

    def picked(value, at, axis):
        return lax.dynamic_index_in_dim(value, at, axis, keepdims=False)

    def exchanged(value, move, count, me, axis):
        return [picked(value, me, axis)] + [
            move(picked(value, me ^ away, axis), away) for away in range(1, count)
        ]

    def halved(value, move, count, me):
        while count > 1:
            count //= 2
            halves = value.reshape((2, count) + value.shape[1:])
            upper = me // count % 2
            sent = move(picked(halves, 1 - upper, 0).astype(low), count)
            value = picked(halves, upper, 0).astype(full) + sent.astype(full)
        return value[0]

    def ready(value):
        first = value[(0,) * value.ndim]
        return first == first

    def added(pieces):
        return functools.reduce(jnp.add, [piece.astype(full) for piece in pieces])

    def placed(pieces, me):
        out = jnp.zeros((len(pieces),) + pieces[0].shape, pieces[0].dtype)
        for away, piece in enumerate(pieces):
            out = lax.dynamic_update_index_in_dim(out, piece, me ^ away, 0)
        return out

    def of_group(value):
        return jnp.concatenate([value] + [over_parts(value, away) for away in range(1, TP)], axis=0)

    count = TP * block
    runs = count // RUN

    def as_columns(vector):
        return vector.reshape(depth, -1)

    starts = (positions.reshape(-1)[::RUN] // RUN).astype(low)
    starts = jnp.pad(starts, (0, depth - starts.shape[0]))
    small = jnp.concatenate(
        [
            as_columns(vector)
            for vector in (
                gain_attention,
                bias_attention,
                gain_feed,
                bias_feed,
                bias_merge,
                bias_reduce,
                bias_joined,
                bias_expand,
                starts,
            )
        ],
        axis=1,
    )
    small = jnp.pad(small, ((0, 0), (0, HD - small.shape[1])))

    def by_head(matrix):
        lead = matrix.shape[:-1]
        split = matrix.reshape(lead + (3, TP, heads, HD))
        queries = split[..., 0, :, :, :].reshape(lead + (TP, span))
        kv = jnp.stack([split[..., 1, :, :, :], split[..., 2, :, :, :]], axis=-2)
        return jnp.concatenate([queries, kv.reshape(lead + (TP, 2 * span))], axis=-1)

    def from_head(matrix):
        lead = matrix.shape[:-2]
        queries = matrix[..., :span].reshape(lead + (1, TP, heads, HD))
        kv = matrix[..., span:].reshape(lead + (TP, heads, 2, HD))
        kv = jnp.moveaxis(kv, -2, len(lead))
        return jnp.concatenate([queries, kv], axis=len(lead)).reshape(lead + (3 * width,))

    expand_parts = weight_expand.reshape(depth, copies, TP, groups * my_units)
    expand_parts = jnp.moveaxis(expand_parts, 2, 0).reshape(TP, depth, part_units)
    parts = jnp.concatenate(
        [
            expand_parts,
            jnp.broadcast_to(weight_merge, (TP, depth, width)),
            jnp.swapaxes(by_head(weight_joined), 0, 1),
            jnp.broadcast_to(small, (TP, depth, HD)),
        ],
        axis=2,
    )
    tokens = jnp.where(ready(parts), tokens, jnp.zeros_like(tokens))
    to_merge, to_joined = part_units, part_units + width
    to_small = 3 * span
    mine = swapped(parts, part_lines).reshape(my_units, -1)
    own_low = tokens.reshape(block, width)
    own_later, _ = lax.optimization_barrier((own_low, mine))
    x_pieces = [own_low, over_parts(own_low, 1)]
    x_pieces += [over_parts(own_later, away) for away in range(2, TP)]
    rows = own_low.astype(full)
    first_rows = mine[:, to_joined:]
    mine = jnp.concatenate([mine[:, :to_joined], weight_reduce], axis=1)
    def in_plane(value):
        value = swapped(jnp.broadcast_to(value, (groups,) + value.shape), group_planes)
        return value.reshape(groups * my_units, -1)

    def of_copies(value):
        return [value] + [over_copies(value, away) for away in range(1, copies)]

    near = in_plane(first_rows)
    row_pieces = of_copies(near)
    rest_pieces = of_copies(in_plane(mine))
    up_low, *_ = lax.optimization_barrier((cotangent, *x_pieces[1:]))
    up_low = up_low.reshape(block, width)
    up_pieces = [up_low] + [over_parts(up_low, away) for away in range(1, TP)]
    came = jnp.arange(width, dtype=jnp.int32)
    row, came_part = came % depth, (came // depth) % TP
    came_group = (came // (depth * TP)) % groups
    came_copy = came // (depth * TP * groups) ^ my_copy
    place_of = ((came_copy * TP + came_part) * groups + came_group) * depth + row
    wanted = jnp.arange(width, dtype=jnp.int32)[:, None]
    order = (place_of[None, :] == wanted).astype(low)
    back_order = (place_of[:, None] == wanted[:, 0]).astype(low)
    source = jnp.arange(3 * width, dtype=jnp.int32)
    unit = jnp.arange(part_units, dtype=jnp.int32)
    unit_group = (unit // my_units) % groups
    unit_copy = unit // (my_units * groups) ^ my_copy
    unit_place = (unit_copy * groups + unit_group) * my_units + unit % my_units
    unit_order = (unit_place[None, :] == unit[:, None]).astype(low)

    unit_back_order = (unit_place[:, None] == unit[None, :]).astype(low)
    head_order = lax.dynamic_slice_in_dim(order, my_part * span, span, 0)

    run_starts = near[:, to_small + 13].reshape(groups, TP, depth)
    run_starts = from_mine(from_mine(run_starts, my_group, 0), my_part, 1)
    k_runs = run_starts[:, :, : block // RUN].astype(jnp.int32).reshape(groups, runs)
    q_runs = k_runs[0]
    places = (q_runs[:, None] * RUN + jnp.arange(RUN, dtype=jnp.int32)).reshape(count)

    half_dims = ROT // 2
    frequency = jnp.exp(jnp.arange(half_dims, dtype=full) * (-2.0 * math.log(10000.0) / ROT))
    angles = frequency[:, None] * places.astype(full)
    cosines, sines = jnp.cos(angles), jnp.sin(angles)
    my_source = picked(by_head(source), my_part, 0)
    queries, kv, first_low, second_low, joined_matrix, small_all = prepare(
        heads, order, my_source[:, None], cosines, sines, x_pieces, row_pieces
    )
    gain_one, _, gain_two, _, merge_shift, reduce_shift = small_all[:6]
    expand_shift = jnp.swapaxes(small_all[9:13], 0, 1)
    expand_shift = picked(expand_shift.reshape(copies, TP, groups * my_units), my_part, 1)
    expand_shift = expand_shift.reshape(-1)
    rank = jnp.sum(q_runs[None, :] < q_runs[:, None], axis=1)
    index = jnp.arange(runs, dtype=jnp.int32)
    q_order = jnp.sum(jnp.where(rank[None, :] == index[:, None], index[None, :], 0), axis=1)
    kv_parts = [kv] + [over_groups(kv, away) for away in range(1, groups)]

    tables = (q_runs, q_order.astype(jnp.int32), k_runs.reshape(-1))
    def sent_halves(value, move, count):
        while count > 1:
            count //= 2
            value = value.reshape((2, -1) + value.shape[1:])
            value = value[0].astype(full) + move(value[1].astype(low), count).astype(full)
        return value

    def over_copies_halved(kept, sent):
        value = kept.astype(full) + over_copies(sent, copies // 2).astype(full)
        return sent_halves(value, over_copies, copies // 2).astype(low)

    def over_plane(value):
        return swapped(value.reshape(groups, my_units, -1), group_planes)

    attended_gradient, merge_matrix, fed, second_slope, feed_sums, *later = feed(
        heads,
        my_part[None].astype(jnp.int32),
        (order, back_order, unit_order, unit_back_order),
        gain_two[None, :],
        expand_shift[None, :],
        second_low,
        x_pieces,
        up_pieces,
        rest_pieces,
    )
    kv_parts, later = lax.optimization_barrier((kv_parts, later))
    later = over_plane(over_copies_halved(*later))

    attended_low, kv_sorted, kv_turned, log_totals, deltas, *branches = attend(
        tables, queries, attended_gradient, merge_matrix, fed, kv_parts
    )
    log_totals, later = lax.optimization_barrier((log_totals, later))
    query_total, kv_totals = attend_back(
        tables, queries, attended_gradient, kv_sorted, kv_turned, log_totals, deltas
    )

    def of_rows(pieces):
        return [pieces[0]] + [over_parts(pieces[away], away) for away in range(1, TP)]

    branches, _ = lax.optimization_barrier((of_rows(branches), query_total))
    branches = added(branches)
    result = (rows + branches + merge_shift + reduce_shift).astype(low)

    attended_then, kv_totals, _, _ = lax.optimization_barrier(
        (attended_low, kv_totals, query_total, result)
    )
    later = jnp.sum(later.astype(full), axis=0)
    gradient_weight_reduce = later[:, part_units:]
    merge_rows = dot(attended_then, jnp.concatenate(up_pieces, axis=0)).astype(low)
    merge_rows = dot(head_order, merge_rows, ((0,), (0,))).astype(low)
    later = later[:, :part_units].astype(low)

    upstream = cotangent.reshape(block, width).astype(full)
    expand_sum = feed_sums[2].reshape(copies, -1)
    expand_sum = jnp.swapaxes(placed_alone(expand_sum, my_part, TP), 0, 1).reshape(width, -1)
    nothing = jnp.zeros((width,), full)
    early = [nothing, nothing, feed_sums[0], feed_sums[1], jnp.sum(upstream, axis=0)]
    early = jnp.stack(early + [nothing] * 3)
    early = jnp.concatenate([early, expand_sum.T], axis=0)
    kv_grads = []
    for half in range(2):
        kept, sent = kv_totals[2 * half : 2 * half + 2]
        kept = kept.astype(full)
        for away in halves_of(groups, half)[2]:
            sent = over_groups(sent, away)
            if kept.shape[0] > 1:
                kept = kept + sent.astype(full)
                middle = kept.shape[0] // 2
                kept, sent = kept[:middle], kept[middle:].astype(low)
        kv_grads += [kept[0], sent[0]]
    final_kept, final_sent, slopes = finish(
        heads,
        my_part[None].astype(jnp.int32),
        back_order,
        place_of[:, None],
        my_source[None, :],
        cosines,
        sines,
        joined_matrix,
        gain_one[None, :],
        early,
        query_total,
        first_low,
        second_slope,
        merge_rows,
        x_pieces,
        kv_grads,
    )
    slopes = swapped(slopes, part_lines)
    gradient_tokens = tokens_gradient(own_low, cotangent.reshape(block, width), slopes)

    final = over_copies_halved(final_kept, final_sent).reshape(groups, my_units, -1)
    final = added(exchanged(final, over_groups, groups, my_group, 0)).astype(low)
    final, _ = lax.optimization_barrier((final, slopes))
    final = jnp.concatenate([final, later], axis=1).reshape(TP, depth, -1)
    final = placed(exchanged(final, over_parts, TP, my_part, 0), my_part)
    to_rest = 3 * span + HD
    gradient_weight_joined = from_head(jnp.swapaxes(final[..., : 3 * span], 0, 1))
    small_total = jnp.sum(final[..., 3 * span : to_rest].astype(full), axis=0)
    gradient_weight_merge = jnp.sum(final[..., to_rest : to_rest + width].astype(full), axis=0)
    gradient_weight_expand = final[..., to_rest + width :]
    gradient_weight_expand = jnp.moveaxis(
        gradient_weight_expand.reshape(TP, depth, copies, groups * my_units), 0, 2
    ).reshape(depth, units)
    gradients = small_total[:, :5].T
    gradient_bias_joined = small_total[:, 5:8].reshape(-1)
    gradient_bias_expand = small_total[:, 8:12].reshape(-1)

    def wide(value):
        return value.astype(full)

    return (
        result.reshape(tokens.shape),
        gradient_tokens.reshape(tokens.shape),
        gradients[0],
        gradients[1],
        gradients[2],
        gradients[3],
        wide(gradient_weight_joined),
        gradient_bias_joined,
        wide(gradient_weight_merge),
        gradients[4],
        wide(gradient_weight_expand),
        gradient_bias_expand,
        wide(gradient_weight_reduce),
        gradients[4],
    )


def placed_alone(value, at, count):
    out = jnp.zeros((count,) + value.shape, value.dtype)
    return lax.dynamic_update_index_in_dim(out, value, at, 0)


def solution(mesh):
    rows = P("dp", "blk", None)
    vector, matrix = P(("dp", "blk")), P(("dp", "blk"), None)
    params = (vector,) * 4 + (matrix, vector) * 4
    return jax.shard_map(
        on_device,
        mesh=mesh,
        in_specs=(rows, P("dp", "blk")) + params + (rows,),
        out_specs=(rows, rows) + params,
        check_vma=False,
    )
```

```python
import functools
import math

import jax
import jax.numpy as jnp
from jax import lax
from jax.experimental import pallas as pl
from jax.experimental.pallas import tpu as pltpu
from jax.sharding import PartitionSpec as P

HD = 64
ROT = 16
TP = 4
RUN = 128
TILE = 2 * RUN
FORWARD_KEYS, FORWARD_REST = 1024, 1024
BACKWARD_KEYS, BACKWARD_REST = 1024, 512
VMEM = 56 * 2**20

norm_eps = 1e-05
masked_score = -1e30
low = jnp.bfloat16
full = jnp.float32


def dot(a, b, dims=((1,), (0,))):
    return lax.dot_general(a, b, (dims, ((), ())), preferred_element_type=full)


def tile_of(tile, q_runs_ref, q_order_ref):
    early, late = q_order_ref[2 * tile], q_order_ref[2 * tile + 1]
    early_run, late_run = q_runs_ref[early], q_runs_ref[late]
    rows = [pl.ds(pl.multiple_of(run * RUN, RUN), RUN) for run in (early, late)]
    column = lax.broadcasted_iota(jnp.int32, (1, TILE), 1)
    places = jnp.where(column < RUN, early_run * RUN + column, late_run * RUN + column - RUN)
    return rows, places, early_run * RUN, late_run * RUN + RUN


def over_keys(step, by_all, by_some, many, few, carry):
    blocks = lax.div(by_all, many)
    carry = lax.fori_loop(0, blocks, functools.partial(step, False, many), carry)
    first = blocks * (many // few)
    last = lax.div(by_some + few - 1, few)
    return lax.fori_loop(first, last, functools.partial(step, True, few), carry)


def columns_of(ref, rows, part=slice(None)):
    return jnp.concatenate([ref[part, at] for at in rows], axis=1)


def hidden(scores, first, places):
    k_places = first + lax.broadcasted_iota(jnp.int32, scores.shape, 0)
    return jnp.where(k_places <= places, scores, masked_score)


def forward_kernel(
    heads, groups, runs, q_runs_ref, q_order_ref, k_runs_ref, q_ref, o_grad_ref, *refs
):
    merge_ref, fed_ref, *kv_refs = refs[: groups + 2]
    out_ref, kv, kv_turned, log_ref, delta_ref, *branch_refs = refs[groups + 2 : -3]
    first_w, state, out_total = refs[-3:]
    pair = 2 * HD

    for source in range(groups):

        def place(run, carry, source=source):
            at = pl.multiple_of(k_runs_ref[source * runs + run] * RUN, RUN)
            columns = kv_refs[source][:, pl.ds(pl.multiple_of(run * RUN, RUN), RUN)]
            kv_turned[:, pl.ds(at, RUN)] = columns
            for head in range(heads):
                part = slice(head * pair, (head + 1) * pair)
                kv[pl.ds(at, RUN), part] = columns[part, :].T
            return carry

        lax.fori_loop(0, runs, place, 0)

    def tile_step(tile, carry):
        rows, places, by_all, by_some = tile_of(tile, q_runs_ref, q_order_ref)
        nothing = jnp.zeros((HD, TILE), low)
        for head in range(heads):
            part = slice(head * HD, (head + 1) * HD)
            first_w[head] = jnp.concatenate([columns_of(q_ref, rows, part), nothing], axis=0)
        state[...] = jnp.full(state.shape, masked_score, full)
        out_total[...] = jnp.zeros_like(out_total)

        def step(hides, size, block, sums):
            at = pl.ds(pl.multiple_of(block * size, size), size)
            new_sums = []
            products = [
                dot(kv[at, head * pair : (head + 1) * pair], first_w[head]) for head in range(heads)
            ]
            for head in range(heads):
                scores = products[head]
                if hides:
                    scores = hidden(scores, block * size, places)
                old_max = state[head : head + 1, :]
                new_max = jnp.maximum(old_max, jnp.max(scores, axis=0, keepdims=True))
                weights = jnp.exp(scores - new_max)
                fading = jnp.exp(old_max - new_max)
                state[head : head + 1, :] = new_max
                new_sums.append(sums[head] * fading + jnp.sum(weights, axis=0, keepdims=True))
                here = slice(head * HD, (head + 1) * HD)
                values = kv_turned[head * pair + HD : (head + 1) * pair, at]
                out_total[here, :] = out_total[here, :] * fading + dot(values, weights.astype(low))
            return tuple(new_sums)

        sums = tuple(jnp.zeros((1, TILE), full) for _ in range(heads))
        sums = over_keys(step, by_all, by_some, FORWARD_KEYS, FORWARD_REST, sums)
        for head in range(heads):
            here = slice(head * HD, (head + 1) * HD)
            attended = out_total[here, :] / sums[head]
            log_total = state[head : head + 1, :] + jnp.log(sums[head])
            o_grad = columns_of(o_grad_ref, rows, here).astype(full)
            delta = jnp.sum(o_grad * attended, axis=0, keepdims=True)
            for half, at in enumerate(rows):
                columns = slice(half * RUN, (half + 1) * RUN)
                out_ref[here, at] = attended[:, columns].astype(low)
                log_ref[head : head + 1, at] = log_total[:, columns]
                delta_ref[head : head + 1, at] = delta[:, columns]
        return carry

    lax.fori_loop(0, q_ref.shape[1] // TILE, tile_step, 0)

    block = branch_refs[0].shape[0]
    for piece, ref in enumerate(branch_refs):
        at = slice(piece * block, (piece + 1) * block)
        branch = dot(out_ref[:, at].T, merge_ref[...]) + fed_ref[at, :]
        ref[...] = branch.astype(ref.dtype)


def halves_of(groups, half):
    steps = [2**k for k in range(groups.bit_length() - 1)]
    steps = steps[::-1] if half else steps
    kept = [0]
    for away in steps[:-1]:
        kept = kept + [source ^ away for source in kept]
    return kept, [source ^ steps[-1] for source in kept], steps[::-1]


def backward_kernel(
    heads,
    groups,
    runs,
    q_runs_ref,
    q_order_ref,
    k_runs_ref,
    q_ref,
    o_grad_ref,
    kv,
    kv_turned,
    log_ref,
    delta_ref,
    q_grad_ref,
    *refs,
):
    kv_grad_refs = refs[:4]
    total, first_w, second_w, q_total = refs[4:]
    pair = 2 * HD
    total[...] = jnp.zeros_like(total)

    def tile_step(tile, carry):
        rows, places, by_all, by_some = tile_of(tile, q_runs_ref, q_order_ref)
        nothing = jnp.zeros((HD, TILE), low)
        for head in range(heads):
            part = slice(head * HD, (head + 1) * HD)
            upper = jnp.concatenate([columns_of(q_ref, rows, part), nothing], axis=0)
            lower = jnp.concatenate([nothing, columns_of(o_grad_ref, rows, part)], axis=0)
            first_w[head, :, :TILE] = upper
            first_w[head, :, TILE:] = lower
            second_w[head, :TILE, :] = upper.T
            second_w[head, TILE:, :] = lower.T
        q_total[...] = jnp.zeros_like(q_total)
        log_totals = columns_of(log_ref, rows)
        deltas = columns_of(delta_ref, rows)

        def step(hides, size, block, carry):
            at = pl.ds(pl.multiple_of(block * size, size), size)
            products = [
                dot(kv[at, head * pair : (head + 1) * pair], first_w[head]) for head in range(heads)
            ]
            for head in range(heads):
                part = slice(head * pair, (head + 1) * pair)
                both = products[head]
                scores = both[:, :TILE]
                if hides:
                    scores = hidden(scores, block * size, places)
                chances = jnp.exp(scores - log_totals[head : head + 1, :])
                score_grad = chances * (both[:, TILE:] - deltas[head : head + 1, :])
                score_grad = score_grad.astype(low)
                joint = jnp.concatenate([score_grad, chances.astype(low)], axis=1)
                total[at, part] += dot(joint, second_w[head])
                here = slice(head * HD, (head + 1) * HD)
                keys = kv_turned[head * pair : head * pair + HD, at]
                q_total[here, :] += dot(keys, score_grad)
            return carry

        over_keys(step, by_all, by_some, BACKWARD_KEYS, BACKWARD_REST, 0)
        for half, at in enumerate(rows):
            q_grad_ref[:, at] = q_total[:, half * RUN : (half + 1) * RUN]
        return carry

    lax.fori_loop(0, q_ref.shape[1] // TILE, tile_step, 0)

    half_runs = runs // 2
    for half in range(2):
        kept, sent, _ = halves_of(groups, half)
        for ref, sources in zip(kv_grad_refs[2 * half : 2 * half + 2], (kept, sent)):
            for slot, source in enumerate(sources):

                def give(run, carry, ref=ref, slot=slot, first=source * runs + half * half_runs):
                    at = pl.multiple_of(k_runs_ref[first + run] * RUN, RUN)
                    columns = pl.ds(pl.multiple_of(run * RUN, RUN), RUN)
                    rows = total[pl.ds(at, RUN), :].astype(low)
                    for head in range(heads):
                        part = slice(head * pair, (head + 1) * pair)
                        ref[slot, part, columns] = rows[:, part].T
                    return carry

                lax.fori_loop(0, half_runs, give, 0)


def attention_call(kernel, name, tables, operands, out_shape, scratch, groups, work):
    width, count = operands[0].shape
    heads, runs = width // HD, count // RUN
    pairs = count * groups * count * heads // 2
    smem = pl.BlockSpec(memory_space=pltpu.SMEM)
    vmem = pl.BlockSpec(memory_space=pltpu.VMEM)
    return pl.pallas_call(
        functools.partial(kernel, heads, groups, runs),
        out_shape=out_shape,
        in_specs=[smem] * len(tables) + [vmem] * len(operands),
        out_specs=tuple([vmem] * len(out_shape)),
        scratch_shapes=scratch,
        compiler_params=pltpu.CompilerParams(vmem_limit_bytes=VMEM),
        cost_estimate=pl.CostEstimate(
            flops=work * pairs,
            bytes_accessed=8 * count * width * groups,
            transcendentals=pairs,
        ),
        name=name,
    )(*tables, *operands)


def pieces_of(block, width):
    kept = jax.ShapeDtypeStruct((block, width), full)
    return (kept,) + (jax.ShapeDtypeStruct((block, width), low),) * (TP - 1)


def attend(tables, queries, o_grads, merge_matrix, fed, kv_parts):
    width, count = queries.shape
    keys = len(kv_parts) * count
    out_shape = (
        jax.ShapeDtypeStruct((width, count), low),
        jax.ShapeDtypeStruct((keys, 2 * width), low),
        jax.ShapeDtypeStruct((2 * width, keys), low),
        jax.ShapeDtypeStruct((8, count), full),
        jax.ShapeDtypeStruct((8, count), full),
    ) + pieces_of(count // TP, fed.shape[1])
    scratch = [
        pltpu.VMEM((width // HD, 2 * HD, TILE), low),
        pltpu.VMEM((8, TILE), full),
        pltpu.VMEM((width, TILE), full),
    ]
    operands = (queries, o_grads, merge_matrix, fed) + tuple(kv_parts)
    groups = len(kv_parts)
    return attention_call(
        forward_kernel, "attend", tables, operands, out_shape, scratch, groups, 6000
    )


def attend_back(tables, queries, o_grads, kv, kv_turned, log_totals, deltas):
    width, count = queries.shape
    keys = kv.shape[0]
    groups = keys // count
    out_shape = (jax.ShapeDtypeStruct((width, count), full),) + (
        jax.ShapeDtypeStruct((groups // 2, 2 * width, count // 2), low),
    ) * 4
    scratch = [
        pltpu.VMEM((keys, 2 * width), full),
        pltpu.VMEM((width // HD, 2 * HD, 2 * TILE), low),
        pltpu.VMEM((width // HD, 2 * TILE, 2 * HD), low),
        pltpu.VMEM((width, TILE), full),
    ]
    operands = (queries, o_grads, kv, kv_turned, log_totals, deltas)
    out = attention_call(
        backward_kernel, "attend_back", tables, operands, out_shape, scratch, groups, 6000
    )
    return out[0], out[1:]


def prepare_kernel(heads, order_ref, source_ref, cosine_ref, sine_ref, *refs):
    x_refs, piece_refs, outs = refs[:TP], refs[TP:-6], refs[-6:]
    q_ref, kv_ref, first_ref, second_ref, matrix_ref, small_ref = outs
    span = heads * HD
    block, width = x_refs[0].shape
    rows = jnp.concatenate([piece[...] for piece in piece_refs], axis=0)
    columns = dot(order_ref[...], rows).astype(low)
    turned_columns = columns.T
    matrix = turned_columns[: 3 * span]
    small = turned_columns[3 * span :].astype(full)
    matrix_ref[...] = matrix
    small_ref[...] = small
    gain_one, shift_one, gain_two, shift_two = (small[k : k + 1] for k in range(4))

    shift = jnp.zeros((3 * span, 1), full)
    lane = lax.broadcasted_iota(jnp.int32, (3 * span, HD), 1)
    feature = lax.broadcasted_iota(jnp.int32, (3 * span, width), 1)
    for k in range(3):
        chosen = (source_ref[...] == 3 * feature + k).astype(full).astype(low)
        found = dot(chosen, columns[:, 3 * span :])
        shift += jnp.sum(jnp.where(lane == 6 + k, found, 0.0), axis=1, keepdims=True)

    cosines, sines = cosine_ref[...], sine_ref[...]
    half_dims = ROT // 2

    def rotated(head, at):
        cosine, sine = cosines[:, at], sines[:, at]
        first, second = head[:half_dims], head[half_dims:ROT]
        return jnp.concatenate(
            [first * cosine - second * sine, second * cosine + first * sine, head[ROT:]], axis=0
        )

    for piece in range(TP):
        at = slice(piece * block, (piece + 1) * block)
        x = x_refs[piece][...].astype(full)
        centred = x - jnp.mean(x, axis=1, keepdims=True)
        spread = jnp.mean(centred * centred, axis=1, keepdims=True)
        normed = centred * lax.rsqrt(spread + norm_eps)
        first_low = (normed * gain_one + shift_one).astype(low)
        first_ref[at, :] = first_low
        second_ref[at, :] = (normed * gain_two + shift_two).astype(low)
        joined = dot(matrix, first_low, ((1,), (1,))) + shift
        for head in range(heads):
            here = slice(head * HD, (head + 1) * HD)
            queries = rotated(joined[here], at).astype(low)
            q_ref[here, at] = queries * jnp.asarray(HD**-0.5, low)
            to_key = span + 2 * head * HD
            to_value = to_key + HD
            kv_ref[2 * head * HD : (2 * head + 1) * HD, at] = rotated(
                joined[to_key:to_value], at
            ).astype(low)
            kv_ref[(2 * head + 1) * HD : (2 * head + 2) * HD, at] = joined[
                to_value : to_value + HD
            ].astype(low)


def prepare(heads, order, source, cosines, sines, x_pieces, row_pieces):
    block, width = x_pieces[0].shape
    count, span = TP * block, heads * HD
    return pl.pallas_call(
        functools.partial(prepare_kernel, heads),
        out_shape=(
            jax.ShapeDtypeStruct((span, count), low),
            jax.ShapeDtypeStruct((2 * span, count), low),
            jax.ShapeDtypeStruct((count, width), low),
            jax.ShapeDtypeStruct((count, width), low),
            jax.ShapeDtypeStruct((3 * span, width), low),
            jax.ShapeDtypeStruct((HD, width), full),
        ),
        compiler_params=pltpu.CompilerParams(vmem_limit_bytes=VMEM),
        cost_estimate=pl.CostEstimate(
            flops=50 * width * span * count, bytes_accessed=16 * count * width, transcendentals=count
        ),
        name="prepare",
    )(order, source, cosines, sines, *x_pieces, *row_pieces)


def feed_kernel(
    heads,
    part_ref,
    order_ref,
    back_order_ref,
    unit_order_ref,
    unit_back_order_ref,
    gain_ref,
    shift_ref,
    second_ref,
    *refs,
):
    x_refs, up_refs, piece_refs, refs = refs[:TP], refs[TP : 2 * TP], refs[2 * TP : -11], refs[-11:]
    o_grad_ref, merge_ref, fed_ref, slope_ref, sums_ref, kept_ref, sent_ref = refs[:7]
    expand, reduce, active, gradient = refs[7:]
    span = heads * HD
    block, width = x_refs[0].shape
    units = expand.shape[1]
    rows = jnp.concatenate([piece[...] for piece in piece_refs], axis=0)
    expand[...] = dot(order_ref[...], rows[:, :units]).astype(low)
    reduce[...] = dot(unit_order_ref[...], rows[:, units + width :]).astype(low)
    mine = pl.ds(pl.multiple_of(part_ref[0] * span, span), span)
    merge_ref[...] = dot(order_ref[mine, :], rows[:, units : units + width]).astype(low)
    sums = [jnp.zeros((1, width), full)] * 2 + [jnp.zeros((1, units), full)]
    for piece in range(TP):
        at = slice(piece * block, (piece + 1) * block)
        up = up_refs[piece][...]
        expanded = dot(second_ref[at, :], expand[...]) + shift_ref[...]
        normal = 0.5 + 0.5 * lax.erf(expanded * 0.5**0.5)
        active_low = (expanded * normal).astype(low)
        active[at, :] = active_low
        fed_ref[at, :] = dot(active_low, reduce[...])
        o_grad_ref[:, at] = dot(merge_ref[...], up, ((1,), (1,))).astype(low)
        density = jnp.exp(-0.5 * expanded * expanded) * (2 * math.pi) ** -0.5
        expanded_gradient = dot(up, reduce[...], ((1,), (1,))) * (normal + expanded * density)
        gradient_low = expanded_gradient.astype(low)
        gradient[at, :] = gradient_low
        sums[2] += jnp.sum(gradient_low.astype(full), axis=0, keepdims=True)
        second_gradient = dot(gradient_low, expand[...], ((1,), (1,)))
        x = x_refs[piece][...].astype(full)
        centred = x - jnp.mean(x, axis=1, keepdims=True)
        spread = jnp.mean(centred * centred, axis=1, keepdims=True)
        normed = centred * lax.rsqrt(spread + norm_eps)
        sums[0] += jnp.sum(second_gradient * normed, axis=0, keepdims=True)
        sums[1] += jnp.sum(second_gradient, axis=0, keepdims=True)
        slope_ref[at, :] = second_gradient * gain_ref[...]
    sums_ref[...] = jnp.concatenate(sums + [jnp.zeros((5, width), full)], axis=0)
    up = jnp.concatenate([ref[...] for ref in up_refs], axis=0)
    expand_rows = dot(second_ref[...].T, gradient[...]).astype(low)
    reduce_rows = dot(active[...].T, up).astype(low)
    expand_rows = dot(back_order_ref[...], expand_rows).astype(low)
    reduce_rows = dot(unit_back_order_ref[...], reduce_rows).astype(low)
    half = width // 2
    for ref, at in ((kept_ref, slice(half)), (sent_ref, slice(half, width))):
        ref[:, :units] = expand_rows[at]
        ref[:, units:] = reduce_rows[at]


def feed(heads, part, orders, gain, shift, second_low, x_pieces, up_pieces, row_pieces):
    block, width = x_pieces[0].shape
    count, span, units = TP * block, heads * HD, shift.shape[1]
    rows_shape = jax.ShapeDtypeStruct((width // 2, units + width), low)
    operands = (*orders, gain, shift, second_low, *x_pieces, *up_pieces, *row_pieces)
    vmem = pl.BlockSpec(memory_space=pltpu.VMEM)
    return pl.pallas_call(
        functools.partial(feed_kernel, heads),
        out_shape=(
            jax.ShapeDtypeStruct((span, count), low),
            jax.ShapeDtypeStruct((span, width), low),
            jax.ShapeDtypeStruct((count, width), full),
            jax.ShapeDtypeStruct((count, width), full),
            jax.ShapeDtypeStruct((8, width), full),
            rows_shape,
            rows_shape,
        ),
        in_specs=[pl.BlockSpec(memory_space=pltpu.SMEM)] + [vmem] * len(operands),
        out_specs=(vmem,) * 7,
        scratch_shapes=[
            pltpu.VMEM((width, units), low),
            pltpu.VMEM((units, width), low),
            pltpu.VMEM((count, units), low),
            pltpu.VMEM((count, units), low),
        ],
        compiler_params=pltpu.CompilerParams(vmem_limit_bytes=VMEM),
        cost_estimate=pl.CostEstimate(flops=0, bytes_accessed=0, transcendentals=0),
        name="feed",
    )(part, *operands)


def finish_kernel(
    heads,
    part_ref,
    order_ref,
    place_ref,
    source_ref,
    cosine_ref,
    sine_ref,
    matrix_ref,
    gain_ref,
    early_ref,
    q_grad_ref,
    first_ref,
    slope_in_ref,
    merge_ref,
    *refs,
):
    x_refs, kv_refs, outs = refs[:TP], refs[TP:-5], refs[-5:]
    kept_ref, sent_ref, slope_ref, gradient, joined = outs
    kv_pairs = (kv_refs[:2], kv_refs[2:])
    span = heads * HD
    block, width = x_refs[0].shape
    half_dims = ROT // 2
    cosine, sine = cosine_ref[...], sine_ref[...]

    def rotated_back(head):
        first, second = head[:half_dims], head[half_dims:ROT]
        return jnp.concatenate(
            [first * cosine + second * sine, second * cosine - first * sine, head[ROT:]], axis=0
        )

    for head in range(heads):
        here = slice(head * HD, (head + 1) * HD)
        joined[here, :] = rotated_back(q_grad_ref[here, :] * HD**-0.5).astype(low)
        key = slice(2 * head * HD, (2 * head + 1) * HD)
        value = slice((2 * head + 1) * HD, (2 * head + 2) * HD)
        key_grad, value_grad = (
            jnp.concatenate(
                [kept[part, :] + sent[part, :].astype(full) for kept, sent in kv_pairs], axis=1
            )
            for part in (key, value)
        )
        to_key = span + 2 * head * HD
        joined[to_key : to_key + HD, :] = rotated_back(key_grad).astype(low)
        joined[to_key + HD : to_key + 2 * HD, :] = value_grad.astype(low)

    gain_sum, shift_sum = jnp.zeros((1, width), full), jnp.zeros((1, width), full)
    gain = gain_ref[...]
    for piece in range(TP):
        at = slice(piece * block, (piece + 1) * block)
        x = x_refs[piece][...].astype(full)
        centred = x - jnp.mean(x, axis=1, keepdims=True)
        spread = jnp.mean(centred * centred, axis=1, keepdims=True)
        normed = centred * lax.rsqrt(spread + norm_eps)
        first_gradient = dot(joined[:, at].T, matrix_ref[...])
        gain_sum += jnp.sum(first_gradient * normed, axis=0, keepdims=True)
        shift_sum += jnp.sum(first_gradient, axis=0, keepdims=True)
        slope = first_gradient * gain + slope_in_ref[at, :]
        slope_ref[part_ref[0] ^ piece] = slope.astype(low)

    gradient[...] = dot(joined[...], first_ref[...]).astype(low)
    order = order_ref[...]
    joined_rows = dot(order, gradient[...], ((1,), (1,))).astype(low)
    sums = jnp.concatenate(
        [gain_sum, shift_sum, early_ref[2:, :], jnp.zeros((HD - early_ref.shape[0], width), full)],
        axis=0,
    )
    sums = dot(order, sums.astype(low), ((1,), (1,)))
    joined_sum = jnp.sum(joined[...].astype(full), axis=1, keepdims=True)
    joined_sum = jnp.broadcast_to(joined_sum, (3 * span, HD)).astype(low)
    lane = lax.broadcasted_iota(jnp.int32, (width, HD), 1)
    for k in range(3):
        chosen = (source_ref[...] == 3 * place_ref[...] + k).astype(full).astype(low)
        sums = jnp.where(lane == 5 + k, dot(chosen, joined_sum), sums)
    half = width // 2
    for ref, at in ((kept_ref, slice(half)), (sent_ref, slice(half, width))):
        ref[:, : 3 * span] = joined_rows[at]
        ref[:, 3 * span : 3 * span + HD] = sums[at].astype(low)
        ref[:, 3 * span + HD :] = merge_ref[at, :]


def finish(
    heads,
    part,
    order,
    place,
    source,
    cosines,
    sines,
    matrix,
    gain,
    early,
    q_grad,
    first_low,
    slope,
    merge_rows,
    x_pieces,
    kv_grads,
):
    block, width = x_pieces[0].shape
    count, span = TP * block, heads * HD
    return pl.pallas_call(
        functools.partial(finish_kernel, heads),
        out_shape=(
            jax.ShapeDtypeStruct((width // 2, 3 * span + HD + width), low),
            jax.ShapeDtypeStruct((width // 2, 3 * span + HD + width), low),
            jax.ShapeDtypeStruct((TP, block, width), low),
        ),
        in_specs=[pl.BlockSpec(memory_space=pltpu.SMEM)]
        + [pl.BlockSpec(memory_space=pltpu.VMEM)] * (12 + TP + len(kv_grads)),
        scratch_shapes=[pltpu.VMEM((3 * span, width), low), pltpu.VMEM((3 * span, count), low)],
        compiler_params=pltpu.CompilerParams(vmem_limit_bytes=36 * 2**20),
        cost_estimate=pl.CostEstimate(
            flops=50 * width * span * count, bytes_accessed=16 * count * width, transcendentals=count
        ),
        name="finish",
    )(
        part,
        order,
        place,
        source,
        cosines,
        sines,
        matrix,
        gain,
        early,
        q_grad,
        first_low,
        slope,
        merge_rows,
        *x_pieces,
        *kv_grads,
    )


def tokens_kernel(x_ref, cotangent_ref, slopes_ref, out_ref):
    x = x_ref[...].astype(full)
    centred = x - jnp.mean(x, axis=1, keepdims=True)
    inverse = lax.rsqrt(jnp.mean(centred * centred, axis=1, keepdims=True) + norm_eps)
    normed = centred * inverse
    slope = functools.reduce(jnp.add, [slopes_ref[part].astype(full) for part in range(TP)])
    slope_mean = jnp.mean(slope, axis=1, keepdims=True)
    along = jnp.mean(slope * normed, axis=1, keepdims=True)
    out_ref[...] = cotangent_ref[...].astype(full) + inverse * (slope - slope_mean - normed * along)


def tokens_gradient(x_low, cotangent, slopes):
    return pl.pallas_call(
        tokens_kernel,
        out_shape=jax.ShapeDtypeStruct(x_low.shape, full),
        compiler_params=pltpu.CompilerParams(vmem_limit_bytes=VMEM),
        name="tokens_gradient",
    )(x_low, cotangent, slopes)


def on_device(
    tokens,
    positions,
    gain_attention,
    bias_attention,
    gain_feed,
    bias_feed,
    weight_joined,
    bias_joined,
    weight_merge,
    bias_merge,
    weight_expand,
    bias_expand,
    weight_reduce,
    bias_reduce,
    cotangent,
):
    seqs, block, width = tokens.shape
    units = weight_expand.shape[1]
    copies = lax.axis_size("dp")
    members = lax.axis_size("blk")
    groups = members // TP
    here = lax.axis_index("blk")
    my_part, my_group, my_copy = here // groups, here % groups, lax.axis_index("dp")
    heads = width // HD // TP
    depth = weight_joined.shape[0]
    part_units = units // TP
    my_units = weight_reduce.shape[0]
    span = heads * HD

    def over_parts(value, away):
        return lax.ppermute(value, "blk", [(i, i ^ (away * groups)) for i in range(members)])

    def over_groups(value, away):
        return lax.ppermute(value, "blk", [(i, i ^ away) for i in range(members)])

    def over_copies(value, away):
        return lax.ppermute(value, "dp", [(i, i ^ away) for i in range(copies)])

    part_lines = [[part * groups + g for part in range(TP)] for g in range(groups)]
    group_planes = [[part * groups + g for g in range(groups)] for part in range(TP)]

    def swapped(value, lines):
        return lax.all_to_all(value, "blk", 0, 0, axis_index_groups=lines, tiled=True)

    def from_mine(value, me, axis):
        count = value.shape[axis]
        bit = 1
        while bit < count:
            split = value.reshape(value.shape[:axis] + (-1, 2, bit) + value.shape[axis + 1 :])
            flipped = jnp.flip(split, axis + 1).reshape(value.shape)
            value = jnp.where(me // bit % 2 == 1, flipped, value)
            bit *= 2
        return value

    def picked(value, at, axis):
        return lax.dynamic_index_in_dim(value, at, axis, keepdims=False)

    def exchanged(value, move, count, me, axis):
        return [picked(value, me, axis)] + [
            move(picked(value, me ^ away, axis), away) for away in range(1, count)
        ]

    def halved(value, move, count, me):
        while count > 1:
            count //= 2
            halves = value.reshape((2, count) + value.shape[1:])
            upper = me // count % 2
            sent = move(picked(halves, 1 - upper, 0).astype(low), count)
            value = picked(halves, upper, 0).astype(full) + sent.astype(full)
        return value[0]

    def ready(value):
        first = value[(0,) * value.ndim]
        return first == first

    def added(pieces):
        return functools.reduce(jnp.add, [piece.astype(full) for piece in pieces])

    def placed(pieces, me):
        out = jnp.zeros((len(pieces),) + pieces[0].shape, pieces[0].dtype)
        for away, piece in enumerate(pieces):
            out = lax.dynamic_update_index_in_dim(out, piece, me ^ away, 0)
        return out

    def of_group(value):
        return jnp.concatenate([value] + [over_parts(value, away) for away in range(1, TP)], axis=0)

    count = TP * block
    runs = count // RUN

    def as_columns(vector):
        return vector.reshape(depth, -1)

    starts = (positions.reshape(-1)[::RUN] // RUN).astype(low)
    starts = jnp.pad(starts, (0, depth - starts.shape[0]))
    small = jnp.concatenate(
        [
            as_columns(vector)
            for vector in (
                gain_attention,
                bias_attention,
                gain_feed,
                bias_feed,
                bias_merge,
                bias_reduce,
                bias_joined,
                bias_expand,
                starts,
            )
        ],
        axis=1,
    )
    small = jnp.pad(small, ((0, 0), (0, HD - small.shape[1])))

    def by_head(matrix):
        lead = matrix.shape[:-1]
        split = matrix.reshape(lead + (3, TP, heads, HD))
        queries = split[..., 0, :, :, :].reshape(lead + (TP, span))
        kv = jnp.stack([split[..., 1, :, :, :], split[..., 2, :, :, :]], axis=-2)
        return jnp.concatenate([queries, kv.reshape(lead + (TP, 2 * span))], axis=-1)

    def from_head(matrix):
        lead = matrix.shape[:-2]
        queries = matrix[..., :span].reshape(lead + (1, TP, heads, HD))
        kv = matrix[..., span:].reshape(lead + (TP, heads, 2, HD))
        kv = jnp.moveaxis(kv, -2, len(lead))
        return jnp.concatenate([queries, kv], axis=len(lead)).reshape(lead + (3 * width,))

    expand_parts = weight_expand.reshape(depth, copies, TP, groups * my_units)
    expand_parts = jnp.moveaxis(expand_parts, 2, 0).reshape(TP, depth, part_units)
    parts = jnp.concatenate(
        [
            expand_parts,
            jnp.broadcast_to(weight_merge, (TP, depth, width)),
            jnp.swapaxes(by_head(weight_joined), 0, 1),
            jnp.broadcast_to(small, (TP, depth, HD)),
        ],
        axis=2,
    )
    tokens = jnp.where(ready(parts), tokens, jnp.zeros_like(tokens))
    to_merge, to_joined = part_units, part_units + width
    to_small = 3 * span
    mine = swapped(parts, part_lines).reshape(my_units, -1)
    own_low = tokens.reshape(block, width)
    own_later, _ = lax.optimization_barrier((own_low, mine))
    x_pieces = [own_low, over_parts(own_low, 1)]
    x_pieces += [over_parts(own_later, away) for away in range(2, TP)]
    rows = own_low.astype(full)
    first_rows = mine[:, to_joined:]
    mine = jnp.concatenate([mine[:, :to_joined], weight_reduce], axis=1)
    def in_plane(value):
        value = swapped(jnp.broadcast_to(value, (groups,) + value.shape), group_planes)
        return value.reshape(groups * my_units, -1)

    def of_copies(value):
        return [value] + [over_copies(value, away) for away in range(1, copies)]

    near = in_plane(first_rows)
    row_pieces = of_copies(near)
    rest_pieces = of_copies(in_plane(mine))
    up_low, *_ = lax.optimization_barrier((cotangent, *x_pieces[1:]))
    up_low = up_low.reshape(block, width)
    up_pieces = [up_low] + [over_parts(up_low, away) for away in range(1, TP)]
    came = jnp.arange(width, dtype=jnp.int32)
    row, came_part = came % depth, (came // depth) % TP
    came_group = (came // (depth * TP)) % groups
    came_copy = came // (depth * TP * groups) ^ my_copy
    place_of = ((came_copy * TP + came_part) * groups + came_group) * depth + row
    wanted = jnp.arange(width, dtype=jnp.int32)[:, None]
    order = (place_of[None, :] == wanted).astype(low)
    back_order = (place_of[:, None] == wanted[:, 0]).astype(low)
    source = jnp.arange(3 * width, dtype=jnp.int32)
    unit = jnp.arange(part_units, dtype=jnp.int32)
    unit_group = (unit // my_units) % groups
    unit_copy = unit // (my_units * groups) ^ my_copy
    unit_place = (unit_copy * groups + unit_group) * my_units + unit % my_units
    unit_order = (unit_place[None, :] == unit[:, None]).astype(low)

    unit_back_order = (unit_place[:, None] == unit[None, :]).astype(low)
    head_order = lax.dynamic_slice_in_dim(order, my_part * span, span, 0)

    run_starts = near[:, to_small + 13].reshape(groups, TP, depth)
    run_starts = from_mine(from_mine(run_starts, my_group, 0), my_part, 1)
    k_runs = run_starts[:, :, : block // RUN].astype(jnp.int32).reshape(groups, runs)
    q_runs = k_runs[0]
    places = (q_runs[:, None] * RUN + jnp.arange(RUN, dtype=jnp.int32)).reshape(count)

    half_dims = ROT // 2
    frequency = jnp.exp(jnp.arange(half_dims, dtype=full) * (-2.0 * math.log(10000.0) / ROT))
    angles = frequency[:, None] * places.astype(full)
    cosines, sines = jnp.cos(angles), jnp.sin(angles)
    my_source = picked(by_head(source), my_part, 0)
    queries, kv, first_low, second_low, joined_matrix, small_all = prepare(
        heads, order, my_source[:, None], cosines, sines, x_pieces, row_pieces
    )
    gain_one, _, gain_two, _, merge_shift, reduce_shift = small_all[:6]
    expand_shift = jnp.swapaxes(small_all[9:13], 0, 1)
    expand_shift = picked(expand_shift.reshape(copies, TP, groups * my_units), my_part, 1)
    expand_shift = expand_shift.reshape(-1)
    rank = jnp.sum(q_runs[None, :] < q_runs[:, None], axis=1)
    index = jnp.arange(runs, dtype=jnp.int32)
    q_order = jnp.sum(jnp.where(rank[None, :] == index[:, None], index[None, :], 0), axis=1)
    kv_parts = [kv] + [over_groups(kv, away) for away in range(1, groups)]

    tables = (q_runs, q_order.astype(jnp.int32), k_runs.reshape(-1))
    def sent_halves(value, move, count):
        while count > 1:
            count //= 2
            value = value.reshape((2, -1) + value.shape[1:])
            value = value[0].astype(full) + move(value[1].astype(low), count).astype(full)
        return value

    def over_copies_halved(kept, sent):
        value = kept.astype(full) + over_copies(sent, copies // 2).astype(full)
        return sent_halves(value, over_copies, copies // 2).astype(low)

    def over_plane(value):
        return swapped(value.reshape(groups, my_units, -1), group_planes)

    attended_gradient, merge_matrix, fed, second_slope, feed_sums, *later = feed(
        heads,
        my_part[None].astype(jnp.int32),
        (order, back_order, unit_order, unit_back_order),
        gain_two[None, :],
        expand_shift[None, :],
        second_low,
        x_pieces,
        up_pieces,
        rest_pieces,
    )
    kv_parts, later = lax.optimization_barrier((kv_parts, later))
    later = over_plane(over_copies_halved(*later))

    attended_low, kv_sorted, kv_turned, log_totals, deltas, *branches = attend(
        tables, queries, attended_gradient, merge_matrix, fed, kv_parts
    )
    log_totals, later = lax.optimization_barrier((log_totals, later))
    query_total, kv_totals = attend_back(
        tables, queries, attended_gradient, kv_sorted, kv_turned, log_totals, deltas
    )

    def of_rows(pieces):
        return [pieces[0]] + [over_parts(pieces[away], away) for away in range(1, TP)]

    branches, _ = lax.optimization_barrier((of_rows(branches), query_total))
    branches = added(branches)
    result = (rows + branches + merge_shift + reduce_shift).astype(low)

    attended_then, kv_totals, _, _ = lax.optimization_barrier(
        (attended_low, kv_totals, query_total, result)
    )
    later = jnp.sum(later.astype(full), axis=0)
    gradient_weight_reduce = later[:, part_units:]
    merge_rows = dot(attended_then, jnp.concatenate(up_pieces, axis=0)).astype(low)
    merge_rows = dot(head_order, merge_rows, ((0,), (0,))).astype(low)
    later = later[:, :part_units].astype(low)

    upstream = cotangent.reshape(block, width).astype(full)
    expand_sum = feed_sums[2].reshape(copies, -1)
    expand_sum = jnp.swapaxes(placed_alone(expand_sum, my_part, TP), 0, 1).reshape(width, -1)
    nothing = jnp.zeros((width,), full)
    early = [nothing, nothing, feed_sums[0], feed_sums[1], jnp.sum(upstream, axis=0)]
    early = jnp.stack(early + [nothing] * 3)
    early = jnp.concatenate([early, expand_sum.T], axis=0)
    kv_grads = []
    for half in range(2):
        kept, sent = kv_totals[2 * half : 2 * half + 2]
        kept = kept.astype(full)
        for away in halves_of(groups, half)[2]:
            sent = over_groups(sent, away)
            if kept.shape[0] > 1:
                kept = kept + sent.astype(full)
                middle = kept.shape[0] // 2
                kept, sent = kept[:middle], kept[middle:].astype(low)
        kv_grads += [kept[0], sent[0]]
    final_kept, final_sent, slopes = finish(
        heads,
        my_part[None].astype(jnp.int32),
        back_order,
        place_of[:, None],
        my_source[None, :],
        cosines,
        sines,
        joined_matrix,
        gain_one[None, :],
        early,
        query_total,
        first_low,
        second_slope,
        merge_rows,
        x_pieces,
        kv_grads,
    )
    slopes = swapped(slopes, part_lines)
    gradient_tokens = tokens_gradient(own_low, cotangent.reshape(block, width), slopes)

    final = over_copies_halved(final_kept, final_sent).reshape(groups, my_units, -1)
    final = added(exchanged(final, over_groups, groups, my_group, 0)).astype(low)
    final, _ = lax.optimization_barrier((final, slopes))
    final = jnp.concatenate([final, later], axis=1).reshape(TP, depth, -1)
    final = placed(exchanged(final, over_parts, TP, my_part, 0), my_part)
    to_rest = 3 * span + HD
    gradient_weight_joined = from_head(jnp.swapaxes(final[..., : 3 * span], 0, 1))
    small_total = jnp.sum(final[..., 3 * span : to_rest].astype(full), axis=0)
    gradient_weight_merge = jnp.sum(final[..., to_rest : to_rest + width].astype(full), axis=0)
    gradient_weight_expand = final[..., to_rest + width :]
    gradient_weight_expand = jnp.moveaxis(
        gradient_weight_expand.reshape(TP, depth, copies, groups * my_units), 0, 2
    ).reshape(depth, units)
    gradients = small_total[:, :5].T
    gradient_bias_joined = small_total[:, 5:8].reshape(-1)
    gradient_bias_expand = small_total[:, 8:12].reshape(-1)

    def wide(value):
        return value.astype(full)

    return (
        result.reshape(tokens.shape),
        gradient_tokens.reshape(tokens.shape),
        gradients[0],
        gradients[1],
        gradients[2],
        gradients[3],
        wide(gradient_weight_joined),
        gradient_bias_joined,
        wide(gradient_weight_merge),
        gradients[4],
        wide(gradient_weight_expand),
        gradient_bias_expand,
        wide(gradient_weight_reduce),
        gradients[4],
    )


def placed_alone(value, at, count):
    out = jnp.zeros((count,) + value.shape, value.dtype)
    return lax.dynamic_update_index_in_dim(out, value, at, 0)


def solution(mesh):
    rows = P("dp", "blk", None)
    vector, matrix = P(("dp", "blk")), P(("dp", "blk"), None)
    params = (vector,) * 4 + (matrix, vector) * 4
    return jax.shard_map(
        on_device,
        mesh=mesh,
        in_specs=(rows, P("dp", "blk")) + params + (rows,),
        out_specs=(rows, rows) + params,
        check_vma=False,
    )
```
